512 devices in a mesh: region: 64 (over y_lo, z, core), member: 8 (over y_hi, x).
Axes of the slice: x: 4, y: 8 (y_hi: 2, y_lo: 4; y = y_hi * 4 + y_lo), z: 8, core: 2. Of those that a mesh axis runs over, the one named last changes fastest.
Arguments:
- prior_state: float32 [80, 15, 16384], P('member', None, 'region'), may hold values from -6 to 6
- observed: float32 [4, 32768], P(None, 'region'), may hold values from -8 to 8
- obs_error: float32 [4, 32768], P(None, 'region'), may hold values from 1.5 to 6
- obs_index: int32 [4, 32768], P(None, 'region'), may hold values from 0 to 3839
- pattern: int32 [4, 64, 3, 4, 2], P(None, 'region'), may hold values 0 or 1
- ancestors: int32 [4, 64, 80], P(None, 'region'), may hold values from 0 to 79
Outputs:
- posterior: float32 [80, 15, 16384], P('member', None, 'region')
The draws below stay inside these ranges and needn't reach their ends.
All inputs are finite; a program needn't handle non-finite values. No bound on the sum of `pattern` on one device may be relied on, other than what follows from the above.
Results may differ from the reference program's by a relative error of at most 0.0003.
Values sent between devices are 32-bit elements; how exact they have to be, the bound alone decides.
A program may use at most 64 MiB of HBM per device.

```python
import math
import jax
import jax.numpy as jnp
from jax import lax

MEMBERS = 80
VARS = 15
CELLS = 256
OBS_DEV = 512
BATCHES = 4
TILE = 128
NCOLS = 16384
NOBS = 32768
OTILES = 4
STILES = 2
N_REGION = 64


def draw_prior_state(key, part):
    key = jax.random.fold_in(key, 23)
    key_base, key_pick, key_size, key_sign = jax.random.split(key, 4)
    regions = NCOLS // CELLS
    base = jax.random.normal(key_base, (MEMBERS, VARS, regions, CELLS), jnp.float32)
    strength = jax.random.uniform(key_size, (regions,), jnp.float32, 2.5, 3.5)
    order = jax.random.permutation(key_pick, regions)
    picked = (order < max(1, regions // 4)).astype(jnp.float32)
    direction = jnp.where(jax.random.bernoulli(key_sign, 0.5, (regions,)), 1.0, -1.0)
    offset = picked * direction * strength
    values = jnp.clip(base + offset[None, None, :, None], -6.0, 6.0)
    return values.reshape(MEMBERS, VARS, NCOLS).astype(jnp.float32)


def draw_observed(key, part):
    key = jax.random.fold_in(key, 11)
    key_noise, key_pick, key_size, key_sign = jax.random.split(key, 4)
    regions = NOBS // OBS_DEV
    noise = 1.5 * jax.random.normal(key_noise, (BATCHES, regions, OBS_DEV), jnp.float32)
    strength = jax.random.uniform(key_size, (BATCHES, regions, 1), jnp.float32, 2.5, 5.0)
    picked = (jax.random.uniform(key_pick, (BATCHES, regions, 1), jnp.float32) < 0.25).astype(jnp.float32)
    direction = jnp.where(jax.random.bernoulli(key_sign, 0.5, (BATCHES, regions, 1)), 1.0, -1.0)
    values = jnp.clip(noise + picked * direction * strength, -8.0, 8.0)
    return values.reshape(BATCHES, NOBS).astype(jnp.float32)


def set_ends(values, rng, least, top_value):
    longest = values.shape.index(max(values.shape))
    spots = []
    for shift in (0, 1):
        where = [jax.random.randint(jax.random.fold_in(rng, axis), (), 0, length) for axis, length in enumerate(values.shape)]
        where[longest] = (where[longest] + shift) % values.shape[longest]
        spots.append(tuple(where))
    return values.at[spots[0]].set(least).at[spots[1]].set(top_value)


def steps_of(rng, dims, cuts, least, high):
    gain = 1.0
    for position, blocks in cuts:
        steps = jax.random.uniform(jax.random.fold_in(jax.random.fold_in(rng, 6), position), (blocks,), jnp.float32, least / len(cuts), high / len(cuts))
        gain = gain * jnp.repeat(jnp.exp(steps), dims[position] // blocks).reshape((-1,) + (1,) * (len(dims) - 1 - position))
    return gain


def setup_inputs(seed: int = 0) -> dict:
    splits = jax.random.split(jax.random.key(seed), 7)
    prior_state = draw_prior_state(jax.random.fold_in(splits[6], 71), 0)
    observed = draw_observed(jax.random.fold_in(splits[6], 71), 0)
    obs_error = jnp.clip(jnp.exp(math.log(6.0) - 1.3862944 * jax.random.uniform(splits[2], (BATCHES, NOBS), jnp.float32) ** steps_of(splits[2], (BATCHES, NOBS), ((1, 64),), -0.2, 0.2)), 1.5, 6.0)
    obs_index = set_ends(jax.random.randint(splits[3], (BATCHES, NOBS), 0, VARS * CELLS), jax.random.fold_in(splits[3], 1), 0, (VARS * CELLS) - 1).astype(jnp.int32)
    pattern = set_ends((jax.random.randint(splits[4], (BATCHES, N_REGION, 3, OTILES, STILES), 0, 3) < 2).astype(jnp.int32), jax.random.fold_in(splits[4], 1), 0, 1)
    ancestors = set_ends(jax.random.randint(splits[5], (BATCHES, N_REGION, MEMBERS), 0, MEMBERS), jax.random.fold_in(splits[5], 1), 0, MEMBERS - 1).astype(jnp.int32)
    return dict(prior_state=prior_state, observed=observed, obs_error=obs_error, obs_index=obs_index, pattern=pattern, ancestors=ancestors)


def local_taper(pattern_block, obs_count, cell_count):
    obs_pos = jnp.arange(3 * obs_count)
    neighbor = obs_pos // obs_count
    within = obs_pos % obs_count
    offset = (neighbor - 1) * cell_count + (within * cell_count) // obs_count
    columns = jnp.arange(cell_count)
    distance = jnp.abs(offset[:, None] - columns[None, :]).astype(jnp.float32)
    taper = jnp.exp(-distance / (0.5 * cell_count))
    blocks = jnp.repeat(jnp.repeat(pattern_block, TILE, axis=1), TILE, axis=2)
    return taper * blocks.reshape(3 * obs_count, cell_count).astype(jnp.float32)


def reference(prior_state, observed, obs_error, obs_index, pattern, ancestors):
    regions = N_REGION
    state = prior_state
    for batch in range(BATCHES):
        blocks = state.reshape(MEMBERS, VARS, regions, CELLS).transpose(2, 0, 1, 3)
        flat = blocks.reshape(regions, MEMBERS, VARS * CELLS)
        obs_cols = obs_index[batch].reshape(regions, 1, OBS_DEV)
        values = jnp.take_along_axis(flat, jnp.broadcast_to(obs_cols, (regions, MEMBERS, OBS_DEV)), axis=2)
        target = observed[batch].reshape(regions, 1, OBS_DEV)
        spread = obs_error[batch].reshape(regions, 1, OBS_DEV)
        misfit = target - values
        terms = -(misfit * misfit) * (0.5 / (spread * spread))
        nearby = jnp.concatenate([jnp.roll(terms, 1, axis=0), terms, jnp.roll(terms, -1, axis=0)], axis=2)
        local_weights = jax.vmap(lambda block: local_taper(block, OBS_DEV, CELLS))(pattern[batch])
        scores = jnp.einsum("rmj,rjc->rmc", nearby, local_weights, precision=lax.Precision.HIGHEST)
        weights = jax.nn.softmax(scores, axis=1)
        post_mean = jnp.einsum("rmc,rmvc->rvc", weights, blocks, precision=lax.Precision.HIGHEST)[:, None]
        chosen = jnp.take_along_axis(blocks, ancestors[batch][:, :, None, None], axis=1)
        updated = post_mean + 0.8 * (chosen - post_mean) + 0.3 * (blocks - post_mean)
        state = updated.transpose(1, 2, 0, 3).reshape(MEMBERS, VARS, regions * CELLS)
    return state
```

```python
import functools

import jax
import jax.numpy as jnp
from jax import lax
from jax.experimental import pallas as pl
from jax.experimental.pallas import tpu as pltpu
from jax.sharding import PartitionSpec as P

MESH = pl.DeviceIdType.MESH
F32, BF16 = jnp.float32, jnp.bfloat16

BATCHES = 4
MEMBERS = 80
GROUP = 8
OWN = 10
VARS = 15
CELLS = 256
OBS = 512
OTILES = 4
ALONG_X = 4
LEFT, RIGHT, SELF = 0, 1, 2


def split2(a):
    hi = a.astype(BF16)
    lo = (a - hi.astype(F32)).astype(BF16)
    return hi, lo


def split3(a):
    hi = a.astype(BF16)
    rest = a - hi.astype(F32)
    mid = rest.astype(BF16)
    lo = (rest - mid.astype(F32)).astype(BF16)
    return hi, mid, lo


def dot(a, b):
    return jnp.dot(a, b, preferred_element_type=F32)


def body(
    regions,
    x_ref, obs_ref, err_ref, idx_ref, pat_ref, anc_ref,
    out_ref,
    xs, xh, lhs, onehot, own_h, ha, hb, ya, yb0, yb1, ha3, hb3, yb03, yb13, xa, xb,
    taper, loc_hi, loc_lo, pe, pe_in, halo_out, halo_in, self_scores, w_all, mean_h, mean_x,
    send, recv,
):
    r = lax.axis_index("region")
    me = lax.axis_index("member")
    along_x = me % ALONG_X
    far = (me + ALONG_X) % GROUP
    base = me - along_x
    far_base = far - along_x

    def beside(step):
        n = r + step
        wrapped = jnp.logical_or(n < 0, n >= regions)
        m = jnp.where(wrapped, far, me)
        return ((n + regions) % regions, m)

    left, right = beside(-1), beside(1)
    partners = [(r, base + (along_x + d) % ALONG_X) for d in (1, 2, 3)]
    across = (r, far)

    def copy(src, dst, sem, device):
        return pltpu.make_async_remote_copy(
            src_ref=src, dst_ref=dst, send_sem=send.at[sem], recv_sem=recv.at[sem],
            device_id=device, device_id_type=MESH,
        )

    barrier = pltpu.get_barrier_semaphore()
    for device in (*partners, across, left, right):
        pl.semaphore_signal(barrier, inc=1, device_id=device, device_id_type=MESH)

    xs[...] = jnp.zeros_like(xs)
    xh[...] = jnp.zeros_like(xh)
    for m in range(OWN):
        x = x_ref[m]
        xs[m, pl.ds(0, VARS), :] = x
        for half in (0, 1):
            xh[half, pl.ds(16 * m, VARS), :] = x[:, 128 * half : 128 * half + 128]
    for v in range(VARS):
        x = jnp.concatenate([xh[half, pl.ds(v, 16, stride=16), :] for half in (0, 1)], axis=1)
        for part, piece in enumerate(split3(x)):
            lhs[pl.ds(part * 16 * VARS + 16 * v, 16), :] = piece

    def sample(b):
        where = idx_ref[pl.ds(b, 1), :]
        var, cell = where // CELLS, where % CELLS
        rows = lax.broadcasted_iota(jnp.int32, (CELLS, OBS), 0)
        onehot[b] = jnp.where(rows == cell, 1.0, 0.0).astype(BF16)
        got = dot(lhs[...], onehot[b])
        n = 16 * VARS
        got = got[:n] + got[n : 2 * n] + got[2 * n :]
        total = jnp.zeros((16, OBS), F32)
        for v in range(VARS):
            total = total + jnp.where(var == v, got[16 * v : 16 * v + 16], 0.0)
        for t in range(OTILES):
            own_h[b // 2, pl.ds(4 * (b % 2) + t, 16, stride=8), :] = total[:, 128 * t : 128 * t + 128]

    def rows_of(member):
        return pl.ds(pl.multiple_of(member * (8 * OWN), 8), 8 * OWN)

    def members_of(member):
        return pl.ds(member * OWN, OWN)

    def gather(src, dst, mine, theirs, sem):
        near = [copy(src, dst.at[mine], sem + i, p) for i, p in enumerate(partners)]
        over = copy(src, dst.at[mine], sem + 3, across)
        block = dst.at[theirs]
        onward = [copy(block, block, sem + 4 + i, p) for i, p in enumerate(partners)]
        return near, over, onward

    sample(0)
    sample(1)
    for b in range(BATCHES):
        for k in range(3):
            p = pat_ref[b, 0, k].astype(F32)
            lane = lax.broadcasted_iota(jnp.int32, (OTILES, CELLS), 1)
            pe[k, pl.ds(4 * b, 4), :] = jnp.where(lane < 128, p[:, 0:1], p[:, 1:2])

    pl.semaphore_wait(barrier, 6)

    gather_a = gather(own_h.at[0, pl.ds(0, 8 * OWN)], ha, rows_of(me), rows_of(far), 0)
    gather_a[1].start()
    for c in gather_a[0]:
        c.start()
    pattern_copies = [
        copy(pe.at[0], pe_in.at[1], 21, left),
        copy(pe.at[2], pe_in.at[0], 22, right),
    ]
    for c in pattern_copies:
        c.start()
    ha[rows_of(me), :] = own_h[0, pl.ds(0, 8 * OWN), :]

    sample(2)
    sample(3)
    gather_b = gather(own_h.at[1, pl.ds(0, 8 * OWN)], hb, rows_of(me), rows_of(far), 7)
    gather_b[1].start()
    for c in gather_b[0]:
        c.start()
    hb[rows_of(me), :] = own_h[1, pl.ds(0, 8 * OWN), :]
    gather_x = gather(xs, xa, members_of(me), members_of(far), 14)
    gather_x[1].start()
    for c in gather_x[0]:
        c.start()
    xa[members_of(me)] = xs[...]

    at = lax.broadcasted_iota(jnp.int32, (OBS, CELLS), 0) // 2
    column = lax.broadcasted_iota(jnp.int32, (OBS, CELLS), 1)
    for dest, shift in ((LEFT, CELLS), (RIGHT, -CELLS), (SELF, 0)):
        distance = jnp.abs(at + shift - column).astype(F32)
        taper[:, CELLS * dest : CELLS * (dest + 1)] = jnp.exp(distance * (-1.0 / (0.5 * CELLS)))

    def localize(b):
        for dest in (LEFT, RIGHT, SELF):
            for t in range(OTILES):
                k = 4 * b + t
                row = pe[1, pl.ds(k, 1), :] if dest == SELF else pe_in[dest, pl.ds(k, 1), :]
                block = (pl.ds(128 * t, 128), pl.ds(CELLS * dest, CELLS))
                loc_hi[block], loc_lo[block] = split2(taper[block] * row)

    for c in pattern_copies:
        c.wait()
    localize(0)

    gather_a[1].wait()
    for c in gather_a[2]:
        c.start()
    for c in (*gather_a[0], *gather_a[2]):
        c.wait()

    y_of = [(ha, hb), (ya, yb0), (None, yb1), (None, yb0)]

    def rows_at(b, batch):
        y = y_of[b][batch // 2]
        return [y[pl.ds(4 * (batch % 2) + t, MEMBERS, stride=8), :] for t in range(OTILES)]

    def terms(b):
        tiles = []
        for t, y in enumerate(rows_at(b, b)):
            lanes = pl.ds(128 * t, 128)
            if b > 0:
                y = y - 0.1 * mean_h[pl.ds(4 * b + t, 1), :]
            miss = obs_ref[pl.ds(b, 1), lanes] - y
            err = err_ref[pl.ds(b, 1), lanes]
            tiles.append(-(miss * miss) * (0.5 / (err * err)))
        return jnp.concatenate(tiles, axis=1)

    def spread(q_hi, q_lo, cols):
        both = dot(jnp.concatenate([q_hi, q_lo], axis=0), loc_hi[:, cols])
        return both[:MEMBERS] + both[MEMBERS:] + dot(q_hi, loc_lo[:, cols])

    def stack(src, dst):
        def step(m, _):
            dst[m] = src[pl.ds(pl.multiple_of(m * 8, 8), 8), :]
            return 0

        lax.fori_loop(0, MEMBERS, step, 0, unroll=8)

    def evolve(b, src, dst, dst3, half):
        old = None if b == 0 else 0.11 * mean_h[pl.ds(8 * half, 8), :]

        def step(m, _):
            y = 0.8 * src[anc_ref[b, 0, m]] + 0.3 * src[m]
            y = y if old is None else y - old
            dst[pl.ds(pl.multiple_of(m * 8, 8), 8), :] = y
            if dst3 is not None:
                dst3[m] = y
            return 0

        lax.fori_loop(0, MEMBERS, step, 0, unroll=8)

    def mean_at(b, batch, w_parts):
        wm = dot(w_parts, onehot[batch])
        wm = wm[:MEMBERS] + wm[MEMBERS:]
        found = []
        for t, y in enumerate(rows_at(b, batch)):
            m = jnp.sum(wm[:, 128 * t : 128 * t + 128] * y, axis=0, keepdims=True)
            if b > 0:
                m = m - 0.1 * mean_h[pl.ds(4 * batch + t, 1), :]
            found.append(m)
        return found

    def store_mean(batch, found):
        for t, m in enumerate(found):
            mean_h[pl.ds(4 * batch + t, 1), :] = m

    def mean_state(b, x):
        def step(m, acc):
            w = w_all[b, pl.ds(m, 1), :]
            return acc + w * x[m]

        return lax.fori_loop(0, MEMBERS, step, jnp.zeros((16, CELLS), F32), unroll=8)

    def advance(b, x, y):
        mean_x[...] = 0.1 * mean_state(b, x)

        def step(m, _):
            y[m] = 0.8 * x[anc_ref[b, 0, m]] + 0.3 * x[m] - mean_x[...]
            return 0

        lax.fori_loop(0, MEMBERS, step, 0, unroll=8)

    w_parts = None
    for b in range(BATCHES):
        q_hi, q_lo = split2(terms(b))
        halo = []
        for dest, device in ((LEFT, left), (RIGHT, right)):
            halo_out[b, dest] = spread(q_hi, q_lo, pl.ds(CELLS * dest, CELLS))
            c = copy(halo_out.at[b, dest], halo_in.at[b, 1 - dest], 23 + 2 * b + dest, device)
            c.start()
            halo.append(c)
        self_scores[...] = spread(q_hi, q_lo, pl.ds(CELLS * SELF, CELLS))

        if b == 0:
            gather_b[1].wait()
            for c in gather_b[2]:
                c.start()
            for c in (*gather_b[0], *gather_b[2]):
                c.wait()
            stack(ha, ha3)
            stack(hb, hb3)
            evolve(0, ha3, ya, None, 0)
            evolve(0, hb3, yb0, yb03, 1)
        if b == 1:
            for batch in (2, 3):
                store_mean(batch, mean_at(0, batch, w_parts))
            evolve(1, yb03, yb1, yb13, 1)
            gather_x[1].wait()
            for c in gather_x[2]:
                c.start()
        if b == 2:
            store_mean(3, mean_at(1, 3, w_parts))
            evolve(2, yb13, yb0, None, 1)
            for c in (*gather_x[0], *gather_x[2]):
                c.wait()
            advance(0, xa, xb)
        if b == 3:
            advance(1, xb, xa)
            advance(2, xa, xb)
        if b + 1 < BATCHES:
            localize(b + 1)

        for c in halo:
            c.wait()
        scores = self_scores[...] + halo_in[b, 0] + halo_in[b, 1]
        raised = jnp.exp(scores - jnp.max(scores, axis=0, keepdims=True))
        weights = raised / jnp.sum(raised, axis=0, keepdims=True)
        w_all[b] = weights
        if b + 1 < BATCHES:
            w_parts = jnp.concatenate(split2(weights), axis=0)
            store_mean(b + 1, mean_at(b, b + 1, w_parts))

    mean = 0.1 * mean_state(BATCHES - 1, xb)
    for i in range(OWN):
        m = me * OWN + i
        x = 0.8 * xb[anc_ref[BATCHES - 1, 0, m]] + 0.3 * xb[m] - mean
        out_ref[i] = x[:VARS]


def local(regions, *args):
    whole = pl.BlockSpec(memory_space=pltpu.VMEM)
    vmem = pltpu.VMEM
    return pl.pallas_call(
        functools.partial(body, regions),
        out_shape=jax.ShapeDtypeStruct((OWN, VARS, CELLS), F32),
        in_specs=[whole] * 5 + [pl.BlockSpec(memory_space=pltpu.SMEM)],
        out_specs=whole,
        scratch_shapes=[
            vmem((OWN, 16, CELLS), F32),
            vmem((2, 256, 128), F32),
            vmem((3 * 16 * VARS, CELLS), BF16),
            vmem((BATCHES, CELLS, OBS), BF16),
            vmem((2, 128, 128), F32),
            vmem((8 * MEMBERS, 128), F32),
            vmem((8 * MEMBERS, 128), F32),
            vmem((8 * MEMBERS, 128), F32),
            vmem((8 * MEMBERS, 128), F32),
            vmem((8 * MEMBERS, 128), F32),
            vmem((MEMBERS, 8, 128), F32),
            vmem((MEMBERS, 8, 128), F32),
            vmem((MEMBERS, 8, 128), F32),
            vmem((MEMBERS, 8, 128), F32),
            vmem((MEMBERS, 16, CELLS), F32),
            vmem((MEMBERS, 16, CELLS), F32),
            vmem((OBS, 3 * CELLS), F32),
            vmem((OBS, 3 * CELLS), BF16),
            vmem((OBS, 3 * CELLS), BF16),
            vmem((3, 4 * BATCHES, CELLS), F32),
            vmem((2, 4 * BATCHES, CELLS), F32),
            vmem((BATCHES, 2, MEMBERS, CELLS), F32),
            vmem((BATCHES, 2, MEMBERS, CELLS), F32),
            vmem((MEMBERS, CELLS), F32),
            vmem((BATCHES, MEMBERS, CELLS), F32),
            vmem((16, 128), F32),
            vmem((16, CELLS), F32),
            pltpu.SemaphoreType.DMA((31,)),
            pltpu.SemaphoreType.DMA((31,)),
        ],
        compiler_params=pltpu.CompilerParams(
            collective_id=0, has_side_effects=True, vmem_limit_bytes=48 << 20
        ),
        name="particle_filter",
    )(*args)


def solution(mesh):
    placed = (
        P("member", None, "region"),
        P(None, "region"),
        P(None, "region"),
        P(None, "region"),
        P(None, "region", None, None, None),
        P(None, "region", None),
    )
    return jax.shard_map(
        functools.partial(local, mesh.shape["region"]),
        mesh=mesh, in_specs=placed, out_specs=P("member", None, "region"), check_vma=False,
    )
```

```python
import functools

import jax
import jax.numpy as jnp
from jax import lax
from jax.experimental import pallas as pl
from jax.experimental.pallas import tpu as pltpu
from jax.sharding import PartitionSpec as P

MESH = pl.DeviceIdType.MESH
F32, BF16 = jnp.float32, jnp.bfloat16

BATCHES = 4
MEMBERS = 80
GROUP = 8
OWN = 10
VARS = 15
CELLS = 256
OBS = 512
OTILES = 4
ALONG_X = 4
Z_CHIPS, EARLY_FAR, EARLY_NEAR = 8, 4, 4


def split2(a):
    hi = a.astype(BF16)
    lo = (a - hi.astype(F32)).astype(BF16)
    return hi, lo


def split3(a):
    hi = a.astype(BF16)
    rest = a - hi.astype(F32)
    mid = rest.astype(BF16)
    lo = (rest - mid.astype(F32)).astype(BF16)
    return hi, mid, lo


def dot(a, b):
    return jnp.dot(a, b, preferred_element_type=F32)


def body(
    regions,
    x_hbm, obs_hbm, err_hbm, idx_hbm, pat_hbm, anc_hbm,
    out_ref,
    x_ref, obs_ref, err_ref, idx_ref, pat_ref, anc_ref,
    xs, xh, lhs, onehot, own_2d, own_h, y10, y20, y30, y11, y21, y31, y22, y32, y33,
    h1, h2, h3, h21, h31, h32, xa, xb,
    taper, loc_hi, loc_lo, reach, land, z_own, z_first, self_own, self_far, s_out, s_in, s_all, z_out, z_in,
    self_scores, w_all, mean_h, mean_x,
    load_sem, send, recv,
):
    r = lax.axis_index("region")
    me = lax.axis_index("member")
    along_x = me % ALONG_X
    far = (me + ALONG_X) % GROUP
    base = me - along_x
    near_half = me // ALONG_X
    z = (r // 2) % Z_CHIPS
    early_far, early_near = z < EARLY_FAR, z < EARLY_NEAR

    def beside(step):
        n = r + step
        wrapped = jnp.logical_or(n < 0, n >= regions)
        n = (n + regions) % regions
        return (n, jnp.where(wrapped, far, me)), (n, me), (n, far)

    (left, left_same, left_far), (right, right_same, right_far) = beside(-1), beside(1)
    partners = [(r, base + (along_x + d) % ALONG_X) for d in (1, 2, 3)]
    across = (r, far)

    def copy(src, dst, sem, device):
        return pltpu.make_async_remote_copy(
            src_ref=src, dst_ref=dst, send_sem=send.at[sem], recv_sem=recv.at[sem],
            device_id=device, device_id_type=MESH,
        )

    barrier = pltpu.get_barrier_semaphore()
    greeted = (across, left_same, right_same, left_far, right_far, *partners)
    for device in greeted:
        pl.semaphore_signal(barrier, inc=1, device_id=device, device_id_type=MESH)

    held = ((idx_hbm, idx_ref), (pat_hbm, pat_ref), (x_hbm, x_ref), (obs_hbm, obs_ref), (err_hbm, err_ref), (anc_hbm, anc_ref))
    loads = [pltpu.make_async_copy(src, dst, load_sem.at[i]) for i, (src, dst) in enumerate(held)]
    for c in loads:
        c.start()

    at = lax.broadcasted_iota(jnp.int32, (OBS, CELLS), 0) // 2
    column = lax.broadcasted_iota(jnp.int32, (OBS, CELLS), 1)
    taper[...] = jnp.exp(jnp.abs(at - column).astype(F32) * (-1.0 / (0.5 * CELLS)))
    at = lax.broadcasted_iota(jnp.int32, (OBS, 128), 0)
    tile = lax.broadcasted_iota(jnp.int32, (OBS, 128), 1)
    away = jnp.where(tile < OTILES, at // 2, CELLS - at // 2).astype(F32)
    held_by = jnp.logical_and(tile < 2 * OTILES, tile % OTILES == at // 128)
    reach[0], reach[1] = split2(jnp.where(held_by, jnp.exp(away * (-1.0 / (0.5 * CELLS))), 0.0))
    for zeroed in (xs, xh, land):
        zeroed[...] = jnp.zeros_like(zeroed)

    def locate(b):
        where = idx_ref[pl.ds(b, 1), :]
        rows = lax.broadcasted_iota(jnp.int32, (CELLS, OBS), 0)
        onehot[b] = jnp.where(rows == where % CELLS, 1.0, 0.0).astype(BF16)

    lane = lax.broadcasted_iota(jnp.int32, (1, CELLS), 1)

    def blocks(b, k, t):
        low, high = (pat_ref[b, 0, k, c, t].astype(F32) for c in (0, 1))
        return jnp.where(lane < 128, low, high)

    def localize(b):
        for t in range(OTILES):
            rows = pl.ds(128 * t, 128)
            loc_hi[rows, :], loc_lo[rows, :] = split2(taper[rows, :] * blocks(b, 1, t))
        lands = []
        for k, gap in ((2, CELLS - lane), (0, lane)):
            factor = jnp.exp(gap.astype(F32) * (-1.0 / (0.5 * CELLS)))
            lands += [factor * blocks(b, k, t) for t in range(OTILES)]
        hi, lo = split2(jnp.concatenate(lands + [jnp.zeros((8, CELLS), F32)], axis=0))
        land[b % 2, 0, pl.ds(0, 16), :], land[b % 2, 1, pl.ds(0, 16), :] = hi, lo

    def product(a, b_hi, b_lo):
        n = a.shape[0]
        hi, lo = split2(a)
        both = dot(jnp.concatenate([hi, lo], axis=0), b_hi)
        return both[:n] + both[n:] + dot(hi, b_lo)

    def own_scores(q):
        return product(q, loc_hi[...], loc_lo[...])

    def beside_sums(q):
        return product(q, reach[0], reach[1])

    def beside_scores(b, from_left, from_right):
        lanes = lax.broadcasted_iota(jnp.int32, from_left.shape, 1)
        return product(jnp.where(lanes < OTILES, from_right, from_left), land[b % 2, 0], land[b % 2, 1])

    loads[0].wait()
    locate(0)
    loads[1].wait()
    localize(0)
    loads[2].wait()
    for m in range(OWN):
        x = x_ref[m]
        xs[m, pl.ds(0, VARS), :] = x
        for half in (0, 1):
            xh[half, pl.ds(16 * m, VARS), :] = x[:, 128 * half : 128 * half + 128]
    for v in range(VARS):
        x = jnp.concatenate([xh[half, pl.ds(v, 16, stride=16), :] for half in (0, 1)], axis=1)
        for part, piece in enumerate(split3(x)):
            lhs[pl.ds(part * 16 * VARS + 16 * v, 16), :] = piece

    def sample(b):
        var = idx_ref[pl.ds(b, 1), :] // CELLS
        got = dot(lhs[...], onehot[b])
        n = 16 * VARS
        got = got[:n] + got[n : 2 * n] + got[2 * n :]
        total = jnp.zeros((16, OBS), F32)
        for v in range(VARS):
            total = total + jnp.where(var == v, got[16 * v : 16 * v + 16], 0.0)
        return total

    def keep_sample(b):
        total = sample(b)
        for t in range(OTILES):
            own_2d[b - 1, pl.ds(t, 16, stride=8), :] = total[:, 128 * t : 128 * t + 128]
        for m in range(OWN):
            own_h[b - 1, m] = own_2d[b - 1, pl.ds(8 * m, OTILES), :]

    def term(b, t, y):
        lanes = pl.ds(128 * t, 128)
        miss = obs_ref[pl.ds(b, 1), lanes] - y
        err = err_ref[pl.ds(b, 1), lanes]
        return -(miss * miss) * (0.5 / (err * err))

    def members_of(member):
        return pl.ds(member * OWN, OWN)

    def gather(src, dst, sem):
        mine, theirs = dst.at[members_of(me)], dst.at[members_of(far)]
        near = [copy(src, mine, sem + i, p) for i, p in enumerate(partners)]
        over = copy(src, mine, sem + 3, across)
        onward = [copy(theirs, theirs, sem + 4 + i, p) for i, p in enumerate(partners)]
        return near, over, onward

    def start(copies):
        for c in copies:
            c.start()

    def wait(copies):
        for c in copies:
            c.wait()

    for c in loads[3:]:
        c.wait()
    first = sample(0)
    q = jnp.concatenate([term(0, t, first[:, 128 * t : 128 * t + 128]) for t in range(OTILES)], axis=1)
    self_own[...] = own_scores(q)
    z_own[...] = beside_sums(q)

    pl.semaphore_wait(barrier, len(greeted))

    first_copies = [
        copy(self_own, self_far, 21, across),
        copy(z_own, z_first.at[1, 1], 22, left_far),
        copy(z_own, z_first.at[0, 1], 23, right_far),
        copy(z_own, z_first.at[1, 0], 24, left_same),
        copy(z_own, z_first.at[0, 0], 25, right_same),
    ]
    start(first_copies)

    held_h = {1: h1, 2: h2, 3: h3}
    samples = {b: gather(own_h.at[b - 1], held_h[b], 35 + 7 * (b - 1)) for b in (1, 2, 3)}
    members = gather(xs, xa, 0)
    for b in (1, 2, 3):
        locate(b)
        keep_sample(b)
        held_h[b][members_of(me)] = own_h[b - 1]
        if b < 3:
            samples[b][1].start()
        start(samples[b][0])

    @pl.when(early_far)
    def _():
        members[1].start()

    @pl.when(early_near)
    def _():
        start(members[0])

    xa[members_of(me)] = xs[...]

    y_of = {(0, 1): y10, (0, 2): y20, (0, 3): y30, (1, 1): y11, (1, 2): y21, (1, 3): y31, (2, 2): y22, (2, 3): y32, (3, 3): y33}
    blocks_of = {(0, 1): h1, (0, 2): h2, (0, 3): h3, (1, 2): h21, (1, 3): h31, (2, 3): h32}

    def rows_at(b, batch):
        return [y_of[b, batch][pl.ds(t, MEMBERS, stride=8), :] for t in range(OTILES)]

    def mean_rows(batch):
        return pl.ds(8 * (batch - 1), OTILES)

    def mean_row(batch, t):
        return pl.ds(8 * (batch - 1) + t, 1)

    def terms(b):
        return jnp.concatenate(
            [term(b, t, y - 0.1 * mean_h[mean_row(b, t), :]) for t, y in enumerate(rows_at(b, b))], axis=1
        )

    def evolve(b, batch):
        src, flat = blocks_of[b, batch], y_of[0, batch] if b == 0 else None
        rows, blocks = y_of[b + 1, batch], blocks_of.get((b + 1, batch))
        old = None if b == 0 else 0.11 * mean_h[mean_rows(batch), :]

        def step(m, _):
            at = pl.ds(pl.multiple_of(m * 8, 8), OTILES)
            now = src[m]
            y = 0.8 * src[anc_ref[b, 0, m]] + 0.3 * now
            y = y if old is None else y - old
            rows[at, :] = y
            if blocks is not None:
                blocks[m] = y
            if flat is not None:
                flat[at, :] = now
            return 0

        lax.fori_loop(0, MEMBERS, step, 0, unroll=8)

    def mean_at(b, batch, w_parts):
        wm = dot(w_parts, onehot[batch])
        wm = wm[:MEMBERS] + wm[MEMBERS:]
        for t, y in enumerate(rows_at(b, batch)):
            m = jnp.sum(wm[:, 128 * t : 128 * t + 128] * y, axis=0, keepdims=True)
            if b > 0:
                m = m - 0.1 * mean_h[mean_row(batch, t), :]
            mean_h[mean_row(batch, t), :] = m

    def mean_state(b, x):
        def step(m, acc):
            w = w_all[b, pl.ds(m, 1), :]
            return acc + w * x[m]

        return lax.fori_loop(0, MEMBERS, step, jnp.zeros((16, CELLS), F32), unroll=8)

    def advance(b, x, y):
        mean_x[...] = 0.1 * mean_state(b, x)

        def step(m, _):
            y[m] = 0.8 * x[anc_ref[b, 0, m]] + 0.3 * x[m] - mean_x[...]
            return 0

        lax.fori_loop(0, MEMBERS, step, 0, unroll=8)

    def weigh(b, scores):
        raised = jnp.exp(scores - jnp.max(scores, axis=0, keepdims=True))
        weights = raised / jnp.sum(raised, axis=0, keepdims=True)
        w_all[b] = weights
        return jnp.concatenate(split2(weights), axis=0)

    samples[1][1].wait()
    start(samples[1][2])
    wait(first_copies)
    samples[3][1].start()

    @pl.when(jnp.logical_not(early_far))
    def _():
        members[1].start()

    sums = beside_scores(
        0,
        jnp.concatenate([z_first[0, 0], z_first[0, 1]], axis=0),
        jnp.concatenate([z_first[1, 0], z_first[1, 1]], axis=0),
    )
    s_out[pl.ds(0, 16), :] = sums[:16] + self_own[...]
    s_out[pl.ds(OWN, OWN), :] = (sums[16:] + self_far[...])[:OWN]
    s_out[pl.ds(2 * OWN, 4), :] = jnp.zeros((4, CELLS), F32)
    s_copies = [copy(s_out, s_in.at[along_x], 26 + i, p) for i, p in enumerate(partners)]
    start(s_copies)
    s_in[along_x] = s_out[...]
    localize(1)
    samples[2][1].wait()
    start(samples[2][2])
    wait((*samples[1][0], *samples[1][2]))
    evolve(0, 1)
    wait(s_copies)
    for half, first in ((0, near_half), (1, 1 - near_half)):
        rows = jnp.concatenate([s_in[i, pl.ds(OWN * half, OWN), :] for i in range(ALONG_X)], axis=0)
        s_all[pl.ds(pl.multiple_of(first * (MEMBERS // 2), 8), MEMBERS // 2), :] = rows

    w_parts = weigh(0, s_all[...])
    mean_at(0, 1, w_parts)

    for b in range(1, BATCHES):
        q = terms(b)
        z_out[b - 1] = beside_sums(q)
        halo = [
            copy(z_out.at[b - 1], z_in.at[b - 1, 1], 27 + 2 * b, left),
            copy(z_out.at[b - 1], z_in.at[b - 1, 0], 28 + 2 * b, right),
        ]
        start(halo)
        self_scores[...] = own_scores(q)

        if b == 1:
            samples[3][1].wait()
            start(samples[3][2])

            @pl.when(jnp.logical_not(early_near))
            def _():
                start(members[0])

            @pl.when(early_far)
            def _():
                members[1].wait()
                start(members[2])

            wait((*samples[2][0], *samples[2][2]))
            evolve(0, 2)
            mean_at(0, 2, w_parts)
            evolve(1, 2)
            held_w = w_parts
        if b == 2:
            @pl.when(jnp.logical_not(early_far))
            def _():
                members[1].wait()
                start(members[2])

            wait((*samples[3][0], *samples[3][2]))
            evolve(0, 3)
            mean_at(0, 3, held_w)
            evolve(1, 3)
            mean_at(1, 3, w_parts)
            evolve(2, 3)
        if b == 3:
            wait((*members[0], *members[2]))
            advance(0, xa, xb)
            advance(1, xb, xa)
            advance(2, xa, xb)
        if b + 1 < BATCHES:
            localize(b + 1)

        wait(halo)
        w_parts = weigh(b, self_scores[...] + beside_scores(b, z_in[b - 1, 0], z_in[b - 1, 1]))
        if b + 1 < BATCHES:
            mean_at(b, b + 1, w_parts)

    mean = 0.1 * mean_state(BATCHES - 1, xb)
    for i in range(OWN):
        m = me * OWN + i
        x = 0.8 * xb[anc_ref[BATCHES - 1, 0, m]] + 0.3 * xb[m] - mean
        out_ref[i] = x[:VARS]


def local(regions, x, observed, obs_error, obs_index, pattern, ancestors):
    whole = pl.BlockSpec(memory_space=pltpu.VMEM)
    vmem = pltpu.VMEM
    return pl.pallas_call(
        functools.partial(body, regions),
        out_shape=jax.ShapeDtypeStruct((OWN, VARS, CELLS), F32),
        in_specs=[pl.BlockSpec(memory_space=pltpu.HBM)] * 6,
        out_specs=whole,
        scratch_shapes=[
            vmem((OWN, VARS, CELLS), F32),
            vmem((BATCHES, OBS), F32),
            vmem((BATCHES, OBS), F32),
            vmem((BATCHES, OBS), jnp.int32),
            pltpu.SMEM((BATCHES, 1, 3, 2, OTILES), jnp.int32),
            pltpu.SMEM((BATCHES, 1, MEMBERS), jnp.int32),
            vmem((OWN, 16, CELLS), F32),
            vmem((2, 256, 128), F32),
            vmem((3 * 16 * VARS, CELLS), BF16),
            vmem((BATCHES, CELLS, OBS), BF16),
            vmem((BATCHES - 1, 128, 128), F32),
            vmem((BATCHES - 1, OWN, OTILES, 128), F32),
            *[vmem((8 * MEMBERS, 128), F32)] * 9,
            *[vmem((MEMBERS, OTILES, 128), F32)] * 6,
            vmem((MEMBERS, 16, CELLS), F32),
            vmem((MEMBERS, 16, CELLS), F32),
            vmem((OBS, CELLS), F32),
            vmem((OBS, CELLS), BF16),
            vmem((OBS, CELLS), BF16),
            vmem((2, OBS, 128), BF16),
            vmem((2, 2, 128, CELLS), BF16),
            vmem((16, 128), F32),
            vmem((2, 2, 16, 128), F32),
            vmem((16, CELLS), F32),
            vmem((16, CELLS), F32),
            vmem((24, CELLS), F32),
            vmem((ALONG_X, 24, CELLS), F32),
            vmem((MEMBERS, CELLS), F32),
            vmem((BATCHES - 1, MEMBERS, 128), F32),
            vmem((BATCHES - 1, 2, MEMBERS, 128), F32),
            vmem((MEMBERS, CELLS), F32),
            vmem((BATCHES, MEMBERS, CELLS), F32),
            vmem((24, 128), F32),
            vmem((16, CELLS), F32),
            pltpu.SemaphoreType.DMA((6,)),
            pltpu.SemaphoreType.DMA((56,)),
            pltpu.SemaphoreType.DMA((56,)),
        ],
        compiler_params=pltpu.CompilerParams(
            collective_id=0, has_side_effects=True, vmem_limit_bytes=56 << 20
        ),
        name="particle_filter",
    )(x, observed, obs_error, obs_index, jnp.swapaxes(pattern, 3, 4), ancestors)


def solution(mesh):
    placed = (
        P("member", None, "region"),
        P(None, "region"),
        P(None, "region"),
        P(None, "region"),
        P(None, "region", None, None, None),
        P(None, "region", None),
    )
    return jax.shard_map(
        functools.partial(local, mesh.shape["region"]),
        mesh=mesh, in_specs=placed, out_specs=P("member", None, "region"), check_vma=False,
    )
```

```python
import functools

import jax
import jax.numpy as jnp
from jax import lax
from jax.experimental import pallas as pl
from jax.experimental.pallas import tpu as pltpu
from jax.sharding import PartitionSpec as P

MESH = pl.DeviceIdType.MESH
F32, BF16 = jnp.float32, jnp.bfloat16

BATCHES = 4
MEMBERS = 80
GROUP = 8
OWN = 10
VARS = 15
CELLS = 256
OBS = 512
OTILES = 4
ALONG_X = 4
Z_CHIPS, EARLY_FAR, EARLY_NEAR = 8, 4, 4
LAST_SENDS = (0, 0)


def split2(a):
    hi = a.astype(BF16)
    lo = (a - hi.astype(F32)).astype(BF16)
    return hi, lo


def split3(a):
    hi = a.astype(BF16)
    rest = a - hi.astype(F32)
    mid = rest.astype(BF16)
    lo = (rest - mid.astype(F32)).astype(BF16)
    return hi, mid, lo


def dot(a, b):
    return jnp.dot(a, b, preferred_element_type=F32)


def body(
    regions,
    x_hbm, obs_hbm, err_hbm, idx_hbm, pat_hbm, anc_hbm,
    out_ref,
    x_ref, obs_ref, err_ref, idx_ref, pat_ref, anc_ref,
    xs, xh, lhs, onehot, own_2d, own_h, y10, y20, y30, y11, y21, y31, y22, y32, y33,
    h1, h2, h3, h21, h31, h32, xa, xb,
    taper, loc, reach, land, z_own, z_first, self_own, self_far, s_out, s_in, s_all, z_out, z_in,
    self_scores, w_all, mean_h, mean_x,
    load_sem, send, recv,
):
    r = lax.axis_index("region")
    me = lax.axis_index("member")
    along_x = me % ALONG_X
    far = (me + ALONG_X) % GROUP
    base = me - along_x
    near_half = me // ALONG_X
    z = (r // 2) % Z_CHIPS
    early_far, last = z < EARLY_FAR, z == Z_CHIPS - 1
    middle = jnp.logical_not(jnp.logical_or(early_far, last))
    early_near = jnp.logical_and(z < EARLY_NEAR, r % (2 * Z_CHIPS) != 0)

    def beside(step):
        n = r + step
        wrapped = jnp.logical_or(n < 0, n >= regions)
        n = (n + regions) % regions
        return (n, jnp.where(wrapped, far, me)), (n, me), (n, far)

    (left, left_same, left_far), (right, right_same, right_far) = beside(-1), beside(1)
    partners = [(r, base + (along_x + d) % ALONG_X) for d in (1, 2, 3)]
    across = (r, far)

    def copy(src, dst, sem, device):
        return pltpu.make_async_remote_copy(
            src_ref=src, dst_ref=dst, send_sem=send.at[sem], recv_sem=recv.at[sem],
            device_id=device, device_id_type=MESH,
        )

    barrier = pltpu.get_barrier_semaphore()
    greeted = (across, left_same, right_same, left_far, right_far, *partners)
    for device in greeted:
        pl.semaphore_signal(barrier, inc=1, device_id=device, device_id_type=MESH)

    held = ((idx_hbm, idx_ref), (pat_hbm, pat_ref), (x_hbm, x_ref), (obs_hbm, obs_ref), (err_hbm, err_ref), (anc_hbm, anc_ref))
    loads = [pltpu.make_async_copy(src, dst, load_sem.at[i]) for i, (src, dst) in enumerate(held)]
    for c in loads:
        c.start()

    at = lax.broadcasted_iota(jnp.int32, (OBS, CELLS), 0) // 2
    column = lax.broadcasted_iota(jnp.int32, (OBS, CELLS), 1)
    taper[...] = jnp.exp(jnp.abs(at - column).astype(F32) * (-1.0 / (0.5 * CELLS)))
    at = lax.broadcasted_iota(jnp.int32, (OBS, 128), 0)
    tile = lax.broadcasted_iota(jnp.int32, (OBS, 128), 1)
    away = jnp.where(tile < OTILES, at // 2, CELLS - at // 2).astype(F32)
    held_by = jnp.logical_and(tile < 2 * OTILES, tile % OTILES == at // 128)
    reach[:, :128], reach[:, 128:] = split2(jnp.where(held_by, jnp.exp(away * (-1.0 / (0.5 * CELLS))), 0.0))
    for zeroed in (xs, xh, land):
        zeroed[...] = jnp.zeros_like(zeroed)

    def locate(b):
        where = idx_ref[pl.ds(b, 1), :]
        rows = lax.broadcasted_iota(jnp.int32, (CELLS, OBS), 0)
        onehot[b] = jnp.where(rows == where % CELLS, 1.0, 0.0).astype(BF16)

    lane = lax.broadcasted_iota(jnp.int32, (1, CELLS), 1)

    def blocks(b, k, t):
        low, high = (pat_ref[b, 0, k, c, t].astype(F32) for c in (0, 1))
        return jnp.where(lane < 128, low, high)

    def localize(b):
        for t in range(OTILES):
            rows = pl.ds(128 * t, 128)
            loc[rows, :CELLS], loc[rows, CELLS:] = split2(taper[rows, :] * blocks(b, 1, t))
        lands = []
        for k, gap in ((2, CELLS - lane), (0, lane)):
            factor = jnp.exp(gap.astype(F32) * (-1.0 / (0.5 * CELLS)))
            lands += [factor * blocks(b, k, t) for t in range(OTILES)]
        hi, lo = split2(jnp.concatenate(lands + [jnp.zeros((8, CELLS), F32)], axis=0))
        land[b % 2, pl.ds(0, 16), :CELLS], land[b % 2, pl.ds(0, 16), CELLS:] = hi, lo

    def product(a, b):
        n, k = a.shape[0], b.shape[1] // 2
        all_four = dot(jnp.concatenate(split2(a), axis=0), b)
        return all_four[:n, :k] + (all_four[n:, :k] + all_four[:n, k:]) + all_four[n:, k:]

    def own_scores(q):
        return product(q, loc[...])

    def beside_sums(q):
        return product(q, reach[...])

    def beside_scores(b, from_left, from_right):
        lanes = lax.broadcasted_iota(jnp.int32, from_left.shape, 1)
        return product(jnp.where(lanes < OTILES, from_right, from_left), land[b % 2])

    loads[0].wait()
    locate(0)
    loads[1].wait()
    localize(0)
    loads[2].wait()
    for m in range(OWN):
        x = x_ref[m]
        xs[m, pl.ds(0, VARS), :] = x
        for half in (0, 1):
            xh[half, pl.ds(16 * m, VARS), :] = x[:, 128 * half : 128 * half + 128]
    for v in range(VARS):
        x = jnp.concatenate([xh[half, pl.ds(v, 16, stride=16), :] for half in (0, 1)], axis=1)
        for part, piece in enumerate(split3(x)):
            lhs[pl.ds(part * 16 * VARS + 16 * v, 16), :] = piece

    def sample(b):
        var = idx_ref[pl.ds(b, 1), :] // CELLS
        got = dot(lhs[...], onehot[b])
        n = 16 * VARS
        got = got[:n] + got[n : 2 * n] + got[2 * n :]
        total = jnp.zeros((16, OBS), F32)
        for v in range(VARS):
            total = total + jnp.where(var == v, got[16 * v : 16 * v + 16], 0.0)
        return total

    def keep_sample(b):
        total = sample(b)
        for t in range(OTILES):
            own_2d[b - 1, pl.ds(t, 16, stride=8), :] = total[:, 128 * t : 128 * t + 128]
        for m in range(OWN):
            own_h[b - 1, m] = own_2d[b - 1, pl.ds(8 * m, OTILES), :]

    def term(b, t, y):
        lanes = pl.ds(128 * t, 128)
        miss = obs_ref[pl.ds(b, 1), lanes] - y
        err = err_ref[pl.ds(b, 1), lanes]
        return -(miss * miss) * (0.5 / (err * err))

    def members_of(member):
        return pl.ds(member * OWN, OWN)

    def gather(src, dst, sem):
        mine, theirs = dst.at[members_of(me)], dst.at[members_of(far)]
        near = [copy(src, mine, sem + i, p) for i, p in enumerate(partners)]
        over = copy(src, mine, sem + 3, across)
        onward = [copy(theirs, theirs, sem + 4 + i, p) for i, p in enumerate(partners)]
        return near, over, onward

    def start(copies):
        for c in copies:
            c.start()

    def arrive(copies):
        for c in copies:
            c.wait_recv()

    def leave(copies):
        for c in copies:
            c.wait_send()

    for c in loads[3:]:
        c.wait()
    first = sample(0)
    q = jnp.concatenate([term(0, t, first[:, 128 * t : 128 * t + 128]) for t in range(OTILES)], axis=1)
    self_own[...] = own_scores(q)
    z_own[...] = beside_sums(q)

    pl.semaphore_wait(barrier, len(greeted))

    first_copies = [
        copy(self_own, self_far, 21, across),
        copy(z_own, z_first.at[1, 1], 22, left_far),
        copy(z_own, z_first.at[0, 1], 23, right_far),
        copy(z_own, z_first.at[1, 0], 24, left_same),
        copy(z_own, z_first.at[0, 0], 25, right_same),
    ]
    start(first_copies)

    held_h = {1: h1, 2: h2, 3: h3}
    samples = {b: gather(own_h.at[b - 1], held_h[b], 35 + 7 * (b - 1)) for b in (1, 2, 3)}
    mine, theirs = members_of(me), members_of(far)
    near = [copy(xs, xa.at[mine], i, p) for i, p in enumerate(partners)]
    halves = (pl.ds(0, 8), pl.ds(8, 8))
    over = [copy(xs.at[:, rows], xa.at[mine, rows], 3 + i, across) for i, rows in enumerate(halves)]
    onward = [
        [copy(xa.at[theirs, rows], xa.at[theirs, rows], 5 + 3 * i + j, p) for j, p in enumerate(partners)]
        for i, rows in enumerate(halves)
    ]

    def send_over(phase):
        now = [c for c, at in zip(over, LAST_SENDS) if at == phase]
        if now:
            @pl.when(last)
            def _():
                start(now)

    def pass_on(parts=(0, 1)):
        for i in parts:
            arrive(over[i : i + 1])
            start(onward[i])

    for b in (1, 2, 3):
        locate(b)
        keep_sample(b)
        held_h[b][members_of(me)] = own_h[b - 1]
        samples[b][1].start()
        start(samples[b][0])

    @pl.when(early_far)
    def _():
        start(over)

    @pl.when(early_near)
    def _():
        start(near)

    send_over(0)

    xa[members_of(me)] = xs[...]

    y_of = {(0, 1): y10, (0, 2): y20, (0, 3): y30, (1, 1): y11, (1, 2): y21, (1, 3): y31, (2, 2): y22, (2, 3): y32, (3, 3): y33}
    blocks_of = {(0, 1): h1, (0, 2): h2, (0, 3): h3, (1, 2): h21, (1, 3): h31, (2, 3): h32}

    def rows_at(b, batch):
        return [y_of[b, batch][pl.ds(t, MEMBERS, stride=8), :] for t in range(OTILES)]

    def mean_rows(batch):
        return pl.ds(8 * (batch - 1), OTILES)

    def mean_row(batch, t):
        return pl.ds(8 * (batch - 1) + t, 1)

    def terms(b):
        return jnp.concatenate(
            [term(b, t, y - 0.1 * mean_h[mean_row(b, t), :]) for t, y in enumerate(rows_at(b, b))], axis=1
        )

    def evolve(b, batch):
        src, flat = blocks_of[b, batch], y_of[0, batch] if b == 0 else None
        rows, blocks = y_of[b + 1, batch], blocks_of.get((b + 1, batch))
        old = None if b == 0 else 0.11 * mean_h[mean_rows(batch), :]

        def step(m, _):
            at = pl.ds(pl.multiple_of(m * 8, 8), OTILES)
            now = src[m]
            y = 0.8 * src[anc_ref[b, 0, m]] + 0.3 * now
            y = y if old is None else y - old
            rows[at, :] = y
            if blocks is not None:
                blocks[m] = y
            if flat is not None:
                flat[at, :] = now
            return 0

        lax.fori_loop(0, MEMBERS, step, 0, unroll=8)

    def mean_at(b, batch, w_parts):
        wm = dot(w_parts, onehot[batch])
        wm = wm[:MEMBERS] + wm[MEMBERS:]
        for t, y in enumerate(rows_at(b, batch)):
            m = jnp.sum(wm[:, 128 * t : 128 * t + 128] * y, axis=0, keepdims=True)
            if b > 0:
                m = m - 0.1 * mean_h[mean_row(batch, t), :]
            mean_h[mean_row(batch, t), :] = m

    def mean_state(b, x):
        def step(m, acc):
            w = w_all[b, pl.ds(m, 1), :]
            return acc + w * x[m]

        return lax.fori_loop(0, MEMBERS, step, jnp.zeros((16, CELLS), F32), unroll=8)

    def advance(b, x, y):
        mean_x[...] = 0.1 * mean_state(b, x)

        def step(m, _):
            y[m] = 0.8 * x[anc_ref[b, 0, m]] + 0.3 * x[m] - mean_x[...]
            return 0

        lax.fori_loop(0, MEMBERS, step, 0, unroll=8)

    def weigh(b, scores):
        raised = jnp.exp(scores - jnp.max(scores, axis=0, keepdims=True))
        weights = raised / jnp.sum(raised, axis=0, keepdims=True)
        w_all[b] = weights
        return jnp.concatenate(split2(weights), axis=0)

    arrive(samples[1][1:2])
    start(samples[1][2])

    arrive(first_copies)

    @pl.when(middle)
    def _():
        start(over)

    send_over(1)

    sums = beside_scores(
        0,
        jnp.concatenate([z_first[0, 0], z_first[0, 1]], axis=0),
        jnp.concatenate([z_first[1, 0], z_first[1, 1]], axis=0),
    )
    s_out[pl.ds(0, 16), :] = sums[:16] + self_own[...]
    s_out[pl.ds(OWN, OWN), :] = (sums[16:] + self_far[...])[:OWN]
    s_out[pl.ds(2 * OWN, 4), :] = jnp.zeros((4, CELLS), F32)
    s_copies = [copy(s_out, s_in.at[along_x], 26 + i, p) for i, p in enumerate(partners)]
    start(s_copies)
    s_in[along_x] = s_out[...]
    localize(1)
    for b in (2, 3):
        arrive(samples[b][1:2])
        start(samples[b][2])

    @pl.when(jnp.logical_not(early_near))
    def _():
        start(near)

    arrive((*samples[1][0], *samples[1][2]))
    evolve(0, 1)
    arrive(s_copies)
    for half, first in ((0, near_half), (1, 1 - near_half)):
        rows = jnp.concatenate([s_in[i, pl.ds(OWN * half, OWN), :] for i in range(ALONG_X)], axis=0)
        s_all[pl.ds(pl.multiple_of(first * (MEMBERS // 2), 8), MEMBERS // 2), :] = rows

    w_parts = weigh(0, s_all[...])
    mean_at(0, 1, w_parts)

    sent = [*first_copies, *s_copies]
    for group in samples.values():
        sent += [*group[0], group[1], *group[2]]
    for b in range(1, BATCHES):
        q = terms(b)
        z_out[b - 1] = beside_sums(q)
        halo = [
            copy(z_out.at[b - 1], z_in.at[b - 1, 1], 27 + 2 * b, left),
            copy(z_out.at[b - 1], z_in.at[b - 1, 0], 28 + 2 * b, right),
        ]
        start(halo)
        self_scores[...] = own_scores(q)

        if b == 1:
            send_over(2)

            @pl.when(early_far)
            def _():
                pass_on()

            arrive((*samples[2][0], *samples[2][2]))
            evolve(0, 2)
            mean_at(0, 2, w_parts)
            evolve(1, 2)
            held_w = w_parts
        if b == 2:
            send_over(3)

            @pl.when(middle)
            def _():
                pass_on()

            arrive((*samples[3][0], *samples[3][2]))
            evolve(0, 3)
            mean_at(0, 3, held_w)
            evolve(1, 3)
            mean_at(1, 3, w_parts)
            evolve(2, 3)

            @pl.when(last)
            def _():
                pass_on([i for i in (0, 1) if LAST_SENDS[i] < 3])
        if b == 3:
            @pl.when(last)
            def _():
                pass_on([i for i in (0, 1) if LAST_SENDS[i] >= 3])

            arrive((*near, *onward[0], *onward[1]))
            advance(0, xa, xb)
            leave((*near, *over, *onward[0], *onward[1]))
            advance(1, xb, xa)
            advance(2, xa, xb)
        if b + 1 < BATCHES:
            localize(b + 1)

        arrive(halo)
        sent += halo
        w_parts = weigh(b, self_scores[...] + beside_scores(b, z_in[b - 1, 0], z_in[b - 1, 1]))
        if b + 1 < BATCHES:
            mean_at(b, b + 1, w_parts)

    mean = 0.1 * mean_state(BATCHES - 1, xb)
    for i in range(OWN):
        m = me * OWN + i
        x = 0.8 * xb[anc_ref[BATCHES - 1, 0, m]] + 0.3 * xb[m] - mean
        out_ref[i] = x[:VARS]
    leave(sent)


def local(regions, x, observed, obs_error, obs_index, pattern, ancestors):
    whole = pl.BlockSpec(memory_space=pltpu.VMEM)
    vmem = pltpu.VMEM
    return pl.pallas_call(
        functools.partial(body, regions),
        out_shape=jax.ShapeDtypeStruct((OWN, VARS, CELLS), F32),
        in_specs=[pl.BlockSpec(memory_space=pltpu.HBM)] * 6,
        out_specs=whole,
        scratch_shapes=[
            vmem((OWN, VARS, CELLS), F32),
            vmem((BATCHES, OBS), F32),
            vmem((BATCHES, OBS), F32),
            vmem((BATCHES, OBS), jnp.int32),
            pltpu.SMEM((BATCHES, 1, 3, 2, OTILES), jnp.int32),
            pltpu.SMEM((BATCHES, 1, MEMBERS), jnp.int32),
            vmem((OWN, 16, CELLS), F32),
            vmem((2, 256, 128), F32),
            vmem((3 * 16 * VARS, CELLS), BF16),
            vmem((BATCHES, CELLS, OBS), BF16),
            vmem((BATCHES - 1, 128, 128), F32),
            vmem((BATCHES - 1, OWN, OTILES, 128), F32),
            *[vmem((8 * MEMBERS, 128), F32)] * 9,
            *[vmem((MEMBERS, OTILES, 128), F32)] * 6,
            vmem((MEMBERS, 16, CELLS), F32),
            vmem((MEMBERS, 16, CELLS), F32),
            vmem((OBS, CELLS), F32),
            vmem((OBS, 2 * CELLS), BF16),
            vmem((OBS, 2 * 128), BF16),
            vmem((2, 128, 2 * CELLS), BF16),
            vmem((16, 128), F32),
            vmem((2, 2, 16, 128), F32),
            vmem((16, CELLS), F32),
            vmem((16, CELLS), F32),
            vmem((24, CELLS), F32),
            vmem((ALONG_X, 24, CELLS), F32),
            vmem((MEMBERS, CELLS), F32),
            vmem((BATCHES - 1, MEMBERS, 128), F32),
            vmem((BATCHES - 1, 2, MEMBERS, 128), F32),
            vmem((MEMBERS, CELLS), F32),
            vmem((BATCHES, MEMBERS, CELLS), F32),
            vmem((24, 128), F32),
            vmem((16, CELLS), F32),
            pltpu.SemaphoreType.DMA((6,)),
            pltpu.SemaphoreType.DMA((56,)),
            pltpu.SemaphoreType.DMA((56,)),
        ],
        compiler_params=pltpu.CompilerParams(
            collective_id=0, has_side_effects=True, vmem_limit_bytes=56 << 20
        ),
        name="particle_filter",
    )(x, observed, obs_error, obs_index, jnp.swapaxes(pattern, 3, 4), ancestors)


def solution(mesh):
    placed = (
        P("member", None, "region"),
        P(None, "region"),
        P(None, "region"),
        P(None, "region"),
        P(None, "region", None, None, None),
        P(None, "region", None),
    )
    return jax.shard_map(
        functools.partial(local, mesh.shape["region"]),
        mesh=mesh, in_specs=placed, out_specs=P("member", None, "region"), check_vma=False,
    )
```

```python
import functools

import jax
import jax.numpy as jnp
from jax import lax
from jax.experimental import pallas as pl
from jax.experimental.pallas import tpu as pltpu
from jax.sharding import PartitionSpec as P

MESH = pl.DeviceIdType.MESH
F32, BF16 = jnp.float32, jnp.bfloat16

BATCHES = 4
MEMBERS = 80
GROUP = 8
OWN = 10
VARS = 15
CELLS = 256
OBS = 512
OTILES = 4
ALONG_X = 4
Z_CHIPS, EARLY_FAR, EARLY_NEAR = 8, 4, 4
PARTS = 4


def split2(a):
    hi = a.astype(BF16)
    lo = (a - hi.astype(F32)).astype(BF16)
    return hi, lo


def split3(a):
    hi = a.astype(BF16)
    rest = a - hi.astype(F32)
    mid = rest.astype(BF16)
    lo = (rest - mid.astype(F32)).astype(BF16)
    return hi, mid, lo


def dot(a, b):
    return jnp.dot(a, b, preferred_element_type=F32)


def body(
    regions,
    x_hbm, obs_hbm, err_hbm, idx_hbm, pat_hbm, anc_hbm,
    out_ref,
    x_ref, obs_ref, err_ref, idx_ref, pat_ref, anc_ref,
    xs, xh, lhs, onehot, own_2d, own_h, y10, y20, y30, y11, y21, y31, y22, y32, y33,
    h1, h2, h3, h21, h31, h32, xa, xb,
    taper, loc, reach, land, z_own, z_first, self_own, self_far, s_out, s_in, s_all, z_out, z_in,
    self_scores, w_all, mean_h, mean_x,
    load_sem, send, recv,
):
    r = lax.axis_index("region")
    me = lax.axis_index("member")
    along_x = me % ALONG_X
    far = (me + ALONG_X) % GROUP
    base = me - along_x
    near_half = me // ALONG_X
    z = (r // 2) % Z_CHIPS
    early_far, last = z < EARLY_FAR, z == Z_CHIPS - 1
    middle = z < 0
    early_near = jnp.logical_and(z < EARLY_NEAR, r % (2 * Z_CHIPS) != 0)

    def beside(step):
        n = r + step
        wrapped = jnp.logical_or(n < 0, n >= regions)
        n = (n + regions) % regions
        return (n, jnp.where(wrapped, far, me)), (n, me), (n, far)

    (left, left_same, left_far), (right, right_same, right_far) = beside(-1), beside(1)
    partners = [(r, base + (along_x + d) % ALONG_X) for d in (1, 2, 3)]
    across = (r, far)

    def copy(src, dst, sem, device):
        return pltpu.make_async_remote_copy(
            src_ref=src, dst_ref=dst, send_sem=send.at[sem], recv_sem=recv.at[sem],
            device_id=device, device_id_type=MESH,
        )

    barrier = pltpu.get_barrier_semaphore()
    greeted = (across, left_same, right_same, left_far, right_far, *partners)
    for device in greeted:
        pl.semaphore_signal(barrier, inc=1, device_id=device, device_id_type=MESH)

    held = ((idx_hbm, idx_ref), (pat_hbm, pat_ref), (x_hbm, x_ref), (obs_hbm, obs_ref), (err_hbm, err_ref), (anc_hbm, anc_ref))
    loads = [pltpu.make_async_copy(src, dst, load_sem.at[i]) for i, (src, dst) in enumerate(held)]
    for c in loads:
        c.start()

    at = lax.broadcasted_iota(jnp.int32, (OBS, CELLS), 0) // 2
    column = lax.broadcasted_iota(jnp.int32, (OBS, CELLS), 1)
    taper[...] = jnp.exp(jnp.abs(at - column).astype(F32) * (-1.0 / (0.5 * CELLS)))
    at = lax.broadcasted_iota(jnp.int32, (OBS, 128), 0)
    tile = lax.broadcasted_iota(jnp.int32, (OBS, 128), 1)
    away = jnp.where(tile < OTILES, at // 2, CELLS - at // 2).astype(F32)
    held_by = jnp.logical_and(tile < 2 * OTILES, tile % OTILES == at // 128)
    reach[:, :128], reach[:, 128:] = split2(jnp.where(held_by, jnp.exp(away * (-1.0 / (0.5 * CELLS))), 0.0))
    for zeroed in (xs, xh):
        zeroed[...] = jnp.zeros_like(zeroed)

    def locate(b):
        where = idx_ref[pl.ds(b, 1), :]
        rows = lax.broadcasted_iota(jnp.int32, (CELLS, OBS), 0)
        onehot[b] = jnp.where(rows == where % CELLS, 1.0, 0.0).astype(BF16)

    lane = lax.broadcasted_iota(jnp.int32, (1, CELLS), 1)

    def blocks(b, k, t):
        low, high = (pat_ref[b, 0, k, c, t].astype(F32) for c in (0, 1))
        return jnp.where(lane < 128, low, high)

    def localize(b):
        for t in range(OTILES):
            rows = pl.ds(128 * t, 128)
            loc[rows, :CELLS], loc[rows, CELLS:] = split2(taper[rows, :] * blocks(b, 1, t))
        lands = []
        for k, gap in ((2, CELLS - lane), (0, lane)):
            factor = jnp.exp(gap.astype(F32) * (-1.0 / (0.5 * CELLS)))
            lands += [factor * blocks(b, k, t) for t in range(OTILES)]
        land[b % 2] = jnp.concatenate(lands, axis=0)

    def product(a, b):
        n, k = a.shape[0], b.shape[1] // 2
        all_four = dot(jnp.concatenate(split2(a), axis=0), b)
        return all_four[:n, :k] + (all_four[n:, :k] + all_four[:n, k:]) + all_four[n:, k:]

    def own_scores(q):
        return product(q, loc[...])

    def beside_sums(q):
        return product(q, reach[...])

    def beside_scores(b, from_left, from_right, start):
        total = start
        for i in range(2 * OTILES):
            sums = (from_right if i < OTILES else from_left)[:, i : i + 1]
            total = total + sums * land[b % 2, pl.ds(i, 1), :]
        return total

    loads[0].wait()
    locate(0)
    loads[1].wait()
    localize(0)
    loads[2].wait()
    for m in range(OWN):
        x = x_ref[m]
        xs[m, pl.ds(0, VARS), :] = x
        for half in (0, 1):
            xh[half, pl.ds(16 * m, VARS), :] = x[:, 128 * half : 128 * half + 128]
    for v in range(VARS):
        x = jnp.concatenate([xh[half, pl.ds(v, 16, stride=16), :] for half in (0, 1)], axis=1)
        for part, piece in enumerate(split3(x)):
            lhs[pl.ds(part * 16 * VARS + 16 * v, 16), :] = piece

    def sample(b):
        var = idx_ref[pl.ds(b, 1), :] // CELLS
        got = dot(lhs[...], onehot[b])
        n = 16 * VARS
        got = got[:n] + got[n : 2 * n] + got[2 * n :]
        total = jnp.zeros((16, OBS), F32)
        for v in range(VARS):
            total = total + jnp.where(var == v, got[16 * v : 16 * v + 16], 0.0)
        return total

    def keep_sample(b):
        total = sample(b)
        for t in range(OTILES):
            own_2d[b - 1, pl.ds(t, 16, stride=8), :] = total[:, 128 * t : 128 * t + 128]
        for m in range(OWN):
            own_h[b - 1, m] = own_2d[b - 1, pl.ds(8 * m, OTILES), :]

    def term(b, t, y):
        lanes = pl.ds(128 * t, 128)
        miss = obs_ref[pl.ds(b, 1), lanes] - y
        err = err_ref[pl.ds(b, 1), lanes]
        return -(miss * miss) * (0.5 / (err * err))

    def members_of(member):
        return pl.ds(member * OWN, OWN)

    def gather(src, dst, sem):
        mine, theirs = dst.at[members_of(me)], dst.at[members_of(far)]
        near = [copy(src, mine, sem + i, p) for i, p in enumerate(partners)]
        over = copy(src, mine, sem + 3, across)
        onward = [copy(theirs, theirs, sem + 4 + i, p) for i, p in enumerate(partners)]
        return near, over, onward

    def start(copies):
        for c in copies:
            c.start()

    def arrive(copies):
        for c in copies:
            c.wait_recv()

    def leave(copies):
        for c in copies:
            c.wait_send()

    for c in loads[3:]:
        c.wait()
    first = sample(0)
    q = jnp.concatenate([term(0, t, first[:, 128 * t : 128 * t + 128]) for t in range(OTILES)], axis=1)
    self_own[...] = own_scores(q)
    z_own[...] = beside_sums(q)

    pl.semaphore_wait(barrier, len(greeted))

    first_copies = [
        copy(self_own, self_far, 21, across),
        copy(z_own, z_first.at[1, 1], 22, left_far),
        copy(z_own, z_first.at[0, 1], 23, right_far),
        copy(z_own, z_first.at[1, 0], 24, left_same),
        copy(z_own, z_first.at[0, 0], 25, right_same),
    ]
    start(first_copies)

    held_h = {1: h1, 2: h2, 3: h3}
    samples = {b: gather(own_h.at[b - 1], held_h[b], 35 + 7 * (b - 1)) for b in (1, 2, 3)}
    near, over, onward = gather(xs, xa, 0)
    for b in (1, 2, 3):
        locate(b)
        keep_sample(b)
        held_h[b][members_of(me)] = own_h[b - 1]
        samples[b][1].start()
        start(samples[b][0])

    @pl.when(jnp.logical_not(middle))
    def _():
        over.start()

    @pl.when(early_near)
    def _():
        start(near)


    xa[members_of(me)] = xs[...]

    y_of = {(0, 1): y10, (0, 2): y20, (0, 3): y30, (1, 1): y11, (1, 2): y21, (1, 3): y31, (2, 2): y22, (2, 3): y32, (3, 3): y33}
    blocks_of = {(0, 1): h1, (0, 2): h2, (0, 3): h3, (1, 2): h21, (1, 3): h31, (2, 3): h32}

    def rows_at(b, batch):
        return [y_of[b, batch][pl.ds(t, MEMBERS, stride=8), :] for t in range(OTILES)]

    def mean_rows(batch):
        return pl.ds(8 * (batch - 1), OTILES)

    def mean_row(batch, t):
        return pl.ds(8 * (batch - 1) + t, 1)

    def terms(b):
        return jnp.concatenate(
            [term(b, t, y - 0.1 * mean_h[mean_row(b, t), :]) for t, y in enumerate(rows_at(b, b))], axis=1
        )

    def evolve(b, batch):
        src, flat = blocks_of[b, batch], y_of[0, batch] if b == 0 else None
        rows, blocks = y_of[b + 1, batch], blocks_of.get((b + 1, batch))
        old = None if b == 0 else 0.11 * mean_h[mean_rows(batch), :]

        def step(m, _):
            at = pl.ds(pl.multiple_of(m * 8, 8), OTILES)
            now = src[m]
            y = 0.8 * src[anc_ref[b, 0, m]] + 0.3 * now
            y = y if old is None else y - old
            rows[at, :] = y
            if blocks is not None:
                blocks[m] = y
            if flat is not None:
                flat[at, :] = now
            return 0

        lax.fori_loop(0, MEMBERS, step, 0, unroll=8)

    def mean_at(b, batch, w_parts):
        wm = dot(w_parts, onehot[batch])
        wm = wm[:MEMBERS] + wm[MEMBERS:]
        for t, y in enumerate(rows_at(b, batch)):
            m = jnp.sum(wm[:, 128 * t : 128 * t + 128] * y, axis=0, keepdims=True)
            if b > 0:
                m = m - 0.1 * mean_h[mean_row(batch, t), :]
            mean_h[mean_row(batch, t), :] = m

    def mean_state(b, x):
        def step(i, parts):
            at = [PARTS * i + j for j in range(PARTS)]
            return tuple(part + w_all[b, pl.ds(m, 1), :] * x[m] for part, m in zip(parts, at))

        parts = lax.fori_loop(0, MEMBERS // PARTS, step, (jnp.zeros((16, CELLS), F32),) * PARTS, unroll=4)
        return (parts[0] + parts[1]) + (parts[2] + parts[3])

    def advance(b, x, y):
        mean_x[...] = 0.1 * mean_state(b, x)

        def step(m, _):
            y[m] = 0.8 * x[anc_ref[b, 0, m]] + 0.3 * x[m] - mean_x[...]
            return 0

        lax.fori_loop(0, MEMBERS, step, 0, unroll=8)

    def weigh(b, scores):
        raised = jnp.exp(scores - jnp.max(scores, axis=0, keepdims=True))
        weights = raised / jnp.sum(raised, axis=0, keepdims=True)
        w_all[b] = weights
        return jnp.concatenate(split2(weights), axis=0)

    arrive(samples[1][1:2])
    start(samples[1][2])

    arrive(first_copies)

    @pl.when(middle)
    def _():
        over.start()

    near_scores, far_scores = (
        beside_scores(0, z_first[0, i], z_first[1, i], own[...]) for i, own in enumerate((self_own, self_far))
    )
    s_out[pl.ds(0, 16), :] = near_scores
    s_out[pl.ds(OWN, OWN), :] = far_scores[:OWN]
    s_out[pl.ds(2 * OWN, 4), :] = jnp.zeros((4, CELLS), F32)
    s_copies = [copy(s_out, s_in.at[along_x], 26 + i, p) for i, p in enumerate(partners)]
    start(s_copies)
    s_in[along_x] = s_out[...]
    localize(1)
    for b in (2, 3):
        arrive(samples[b][1:2])
        start(samples[b][2])

    arrive((*samples[1][0], *samples[1][2]))
    evolve(0, 1)
    arrive(s_copies)
    @pl.when(jnp.logical_not(early_near))
    def _():
        start(near)

    for half, first in ((0, near_half), (1, 1 - near_half)):
        rows = jnp.concatenate([s_in[i, pl.ds(OWN * half, OWN), :] for i in range(ALONG_X)], axis=0)
        s_all[pl.ds(pl.multiple_of(first * (MEMBERS // 2), 8), MEMBERS // 2), :] = rows

    w_parts = weigh(0, s_all[...])
    mean_at(0, 1, w_parts)

    sent = [*first_copies, *s_copies]
    for group in samples.values():
        sent += [*group[0], group[1], *group[2]]
    for b in range(1, BATCHES):
        q = terms(b)
        z_out[b - 1] = beside_sums(q)
        halo = [
            copy(z_out.at[b - 1], z_in.at[b - 1, 1], 27 + 2 * b, left),
            copy(z_out.at[b - 1], z_in.at[b - 1, 0], 28 + 2 * b, right),
        ]
        start(halo)
        self_scores[...] = own_scores(q)

        if b == 1:
            @pl.when(early_far)
            def _():
                over.wait_recv()
                start(onward)

            arrive((*samples[2][0], *samples[2][2]))
            evolve(0, 2)
            mean_at(0, 2, w_parts)
            evolve(1, 2)
            held_w = w_parts

            @pl.when(jnp.logical_not(early_far))
            def _():
                over.wait_recv()
                start(onward)
        if b == 2:
            @pl.when(middle)
            def _():
                over.wait_recv()
                start(onward)

            arrive((*samples[3][0], *samples[3][2]))
            evolve(0, 3)
            mean_at(0, 3, held_w)
            evolve(1, 3)
            mean_at(1, 3, w_parts)
            evolve(2, 3)
        if b == 3:
            arrive((*near, *onward))
            advance(0, xa, xb)
            leave((*near, over, *onward))
            advance(1, xb, xa)
            advance(2, xa, xb)
            for i in range(OWN):
                m = me * OWN + i
                xs[i] = 0.8 * xb[anc_ref[b, 0, m]] + 0.3 * xb[m]
        if b + 1 < BATCHES:
            localize(b + 1)

        arrive(halo)
        sent += halo
        w_parts = weigh(b, beside_scores(b, z_in[b - 1, 0], z_in[b - 1, 1], self_scores[...]))
        if b + 1 < BATCHES:
            mean_at(b, b + 1, w_parts)

    mean = 0.1 * mean_state(BATCHES - 1, xb)
    for i in range(OWN):
        out_ref[i] = xs[i, pl.ds(0, VARS), :] - mean[:VARS]
    leave(sent)


def local(regions, x, observed, obs_error, obs_index, pattern, ancestors):
    whole = pl.BlockSpec(memory_space=pltpu.VMEM)
    vmem = pltpu.VMEM
    return pl.pallas_call(
        functools.partial(body, regions),
        out_shape=jax.ShapeDtypeStruct((OWN, VARS, CELLS), F32),
        in_specs=[pl.BlockSpec(memory_space=pltpu.HBM)] * 6,
        out_specs=whole,
        scratch_shapes=[
            vmem((OWN, VARS, CELLS), F32),
            vmem((BATCHES, OBS), F32),
            vmem((BATCHES, OBS), F32),
            vmem((BATCHES, OBS), jnp.int32),
            pltpu.SMEM((BATCHES, 1, 3, 2, OTILES), jnp.int32),
            pltpu.SMEM((BATCHES, 1, MEMBERS), jnp.int32),
            vmem((OWN, 16, CELLS), F32),
            vmem((2, 256, 128), F32),
            vmem((3 * 16 * VARS, CELLS), BF16),
            vmem((BATCHES, CELLS, OBS), BF16),
            vmem((BATCHES - 1, 128, 128), F32),
            vmem((BATCHES - 1, OWN, OTILES, 128), F32),
            *[vmem((8 * MEMBERS, 128), F32)] * 9,
            *[vmem((MEMBERS, OTILES, 128), F32)] * 6,
            vmem((MEMBERS, 16, CELLS), F32),
            vmem((MEMBERS, 16, CELLS), F32),
            vmem((OBS, CELLS), F32),
            vmem((OBS, 2 * CELLS), BF16),
            vmem((OBS, 2 * 128), BF16),
            vmem((2, 2 * OTILES, CELLS), F32),
            vmem((16, 128), F32),
            vmem((2, 2, 16, 128), F32),
            vmem((16, CELLS), F32),
            vmem((16, CELLS), F32),
            vmem((24, CELLS), F32),
            vmem((ALONG_X, 24, CELLS), F32),
            vmem((MEMBERS, CELLS), F32),
            vmem((BATCHES - 1, MEMBERS, 128), F32),
            vmem((BATCHES - 1, 2, MEMBERS, 128), F32),
            vmem((MEMBERS, CELLS), F32),
            vmem((BATCHES, MEMBERS, CELLS), F32),
            vmem((24, 128), F32),
            vmem((16, CELLS), F32),
            pltpu.SemaphoreType.DMA((6,)),
            pltpu.SemaphoreType.DMA((56,)),
            pltpu.SemaphoreType.DMA((56,)),
        ],
        compiler_params=pltpu.CompilerParams(
            collective_id=0, has_side_effects=True, vmem_limit_bytes=56 << 20
        ),
        name="particle_filter",
    )(x, observed, obs_error, obs_index, jnp.swapaxes(pattern, 3, 4), ancestors)


def solution(mesh):
    placed = (
        P("member", None, "region"),
        P(None, "region"),
        P(None, "region"),
        P(None, "region"),
        P(None, "region", None, None, None),
        P(None, "region", None),
    )
    return jax.shard_map(
        functools.partial(local, mesh.shape["region"]),
        mesh=mesh, in_specs=placed, out_specs=P("member", None, "region"), check_vma=False,
    )
```

```python
import functools

import jax
import jax.numpy as jnp
from jax import lax
from jax.experimental import pallas as pl
from jax.experimental.pallas import tpu as pltpu
from jax.sharding import PartitionSpec as P

MESH = pl.DeviceIdType.MESH
F32, BF16 = jnp.float32, jnp.bfloat16

BATCHES = 4
MEMBERS = 80
GROUP = 8
OWN = 10
VARS = 15
CELLS = 256
OBS = 512
OTILES = 4
ALONG_X = 4
Z_CHIPS, EARLY_FAR, EARLY_NEAR = 8, 4, 4
PARTS = 4


def split2(a):
    hi = a.astype(BF16)
    lo = (a - hi.astype(F32)).astype(BF16)
    return hi, lo


def split3(a):
    hi = a.astype(BF16)
    rest = a - hi.astype(F32)
    mid = rest.astype(BF16)
    lo = (rest - mid.astype(F32)).astype(BF16)
    return hi, mid, lo


def dot(a, b):
    return jnp.dot(a, b, preferred_element_type=F32)


def body(
    regions,
    x_hbm, obs_hbm, err_hbm, idx_hbm, pat_hbm, anc_hbm,
    out_ref,
    x_ref, obs_ref, err_ref, idx_ref, pat_ref, anc_ref,
    xs, xh, lhs, onehot, own_2d, own_h, y10, y20, y30, y11, y21, y31, y22, y32, y33,
    h1, h2, h3, h21, h31, h32, xa, xb,
    taper, loc, reach, land, z_own, z_first, self_own, self_far, s_out, s_in, s_all, z_out, z_in,
    self_scores, w_all, mean_h, mean_x,
    load_sem, send, recv,
):
    r = lax.axis_index("region")
    me = lax.axis_index("member")
    along_x = me % ALONG_X
    far = (me + ALONG_X) % GROUP
    base = me - along_x
    near_half = me // ALONG_X
    z = (r // 2) % Z_CHIPS
    early_far, last = z < EARLY_FAR, z == Z_CHIPS - 1
    middle = z < 0
    early_near = jnp.logical_and(z < EARLY_NEAR, r % (2 * Z_CHIPS) != 0)

    def beside(step):
        n = r + step
        wrapped = jnp.logical_or(n < 0, n >= regions)
        n = (n + regions) % regions
        return (n, jnp.where(wrapped, far, me)), (n, me), (n, far)

    (left, left_same, left_far), (right, right_same, right_far) = beside(-1), beside(1)
    partners = [(r, base + (along_x + d) % ALONG_X) for d in (1, 2, 3)]
    across = (r, far)

    def copy(src, dst, sem, device):
        return pltpu.make_async_remote_copy(
            src_ref=src, dst_ref=dst, send_sem=send.at[sem], recv_sem=recv.at[sem],
            device_id=device, device_id_type=MESH,
        )

    barrier = pltpu.get_barrier_semaphore()
    greeted = (across, left_same, right_same, left_far, right_far, *partners)
    for device in greeted:
        pl.semaphore_signal(barrier, inc=1, device_id=device, device_id_type=MESH)

    held = ((idx_hbm, idx_ref), (pat_hbm, pat_ref), (x_hbm, x_ref), (obs_hbm, obs_ref), (err_hbm, err_ref), (anc_hbm, anc_ref))
    loads = [pltpu.make_async_copy(src, dst, load_sem.at[i]) for i, (src, dst) in enumerate(held)]
    for c in loads:
        c.start()

    at = lax.broadcasted_iota(jnp.int32, (OBS, CELLS), 0) // 2
    column = lax.broadcasted_iota(jnp.int32, (OBS, CELLS), 1)
    taper[...] = jnp.exp(jnp.abs(at - column).astype(F32) * (-1.0 / (0.5 * CELLS)))
    at = lax.broadcasted_iota(jnp.int32, (OBS, 128), 0)
    tile = lax.broadcasted_iota(jnp.int32, (OBS, 128), 1) % (2 * OTILES)
    away = jnp.where(tile < OTILES, at // 2, CELLS - at // 2).astype(F32)
    held_by = tile % OTILES == at // 128
    reach[:, :128], reach[:, 128:] = split2(jnp.where(held_by, jnp.exp(away * (-1.0 / (0.5 * CELLS))), 0.0))
    for zeroed in (xs, xh):
        zeroed[...] = jnp.zeros_like(zeroed)

    def locate(b):
        where = idx_ref[pl.ds(b, 1), :]
        rows = lax.broadcasted_iota(jnp.int32, (CELLS, OBS), 0)
        onehot[b] = jnp.where(rows == where % CELLS, 1.0, 0.0).astype(BF16)

    lane = lax.broadcasted_iota(jnp.int32, (1, CELLS), 1)

    def blocks(b, k, t):
        low, high = (pat_ref[b, 0, k, c, t].astype(F32) for c in (0, 1))
        return jnp.where(lane < 128, low, high)

    def localize(b):
        for t in range(OTILES):
            rows = pl.ds(128 * t, 128)
            loc[rows, :CELLS], loc[rows, CELLS:] = split2(taper[rows, :] * blocks(b, 1, t))
        lands = []
        for k, gap in ((2, CELLS - lane), (0, lane)):
            factor = jnp.exp(gap.astype(F32) * (-1.0 / (0.5 * CELLS)))
            lands += [factor * blocks(b, k, t) for t in range(OTILES)]
        land[b % 2] = jnp.concatenate(lands, axis=0)

    def product(a, b):
        n, k = a.shape[0], b.shape[1] // 2
        all_four = dot(jnp.concatenate(split2(a), axis=0), b)
        return all_four[:n, :k] + (all_four[n:, :k] + all_four[:n, k:]) + all_four[n:, k:]

    def own_scores(q):
        return product(q, loc[...])

    def beside_sums(q):
        sums = product(q, reach[...])
        held = lax.broadcasted_iota(jnp.int32, (8, 128), 1) // 8
        packed = jnp.zeros((8, 128), F32)
        for g in range(q.shape[0] // 8):
            packed = jnp.where(held == g, sums[8 * g : 8 * g + 8], packed)
        return packed

    def beside_scores(b, from_left, from_right, start):
        found = []
        for g in range(start.shape[0] // 8):
            total = start[8 * g : 8 * g + 8]
            for i in range(2 * OTILES):
                sums = (from_right if i < OTILES else from_left)[:, 8 * g + i : 8 * g + i + 1]
                total = total + sums * land[b % 2, pl.ds(i, 1), :]
            found.append(total)
        return jnp.concatenate(found, axis=0)

    loads[0].wait()
    locate(0)
    loads[1].wait()
    localize(0)
    loads[2].wait()
    for m in range(OWN):
        x = x_ref[m]
        xs[m, pl.ds(0, VARS), :] = x
        for half in (0, 1):
            xh[half, pl.ds(16 * m, VARS), :] = x[:, 128 * half : 128 * half + 128]
    for v in range(VARS):
        x = jnp.concatenate([xh[half, pl.ds(v, 16, stride=16), :] for half in (0, 1)], axis=1)
        for part, piece in enumerate(split3(x)):
            lhs[pl.ds(part * 16 * VARS + 16 * v, 16), :] = piece

    def sample(b):
        var = idx_ref[pl.ds(b, 1), :] // CELLS
        got = dot(lhs[...], onehot[b])
        n = 16 * VARS
        got = got[:n] + got[n : 2 * n] + got[2 * n :]
        total = jnp.zeros((16, OBS), F32)
        for v in range(VARS):
            total = total + jnp.where(var == v, got[16 * v : 16 * v + 16], 0.0)
        return total

    def keep_sample(b):
        total = sample(b)
        for t in range(OTILES):
            own_2d[b - 1, pl.ds(t, 16, stride=8), :] = total[:, 128 * t : 128 * t + 128]
        for m in range(OWN):
            own_h[b - 1, m] = own_2d[b - 1, pl.ds(8 * m, OTILES), :]

    def term(b, t, y):
        lanes = pl.ds(128 * t, 128)
        miss = obs_ref[pl.ds(b, 1), lanes] - y
        err = err_ref[pl.ds(b, 1), lanes]
        return -(miss * miss) * (0.5 / (err * err))

    def members_of(member):
        return pl.ds(member * OWN, OWN)

    def gather(src, dst, sem):
        mine, theirs = dst.at[members_of(me)], dst.at[members_of(far)]
        near = [copy(src, mine, sem + i, p) for i, p in enumerate(partners)]
        over = copy(src, mine, sem + 3, across)
        onward = [copy(theirs, theirs, sem + 4 + i, p) for i, p in enumerate(partners)]
        return near, over, onward

    def start(copies):
        for c in copies:
            c.start()

    def arrive(copies):
        for c in copies:
            c.wait_recv()

    def leave(copies):
        for c in copies:
            c.wait_send()

    for c in loads[3:]:
        c.wait()
    first = sample(0)
    q = jnp.concatenate([term(0, t, first[:, 128 * t : 128 * t + 128]) for t in range(OTILES)], axis=1)
    self_own[...] = own_scores(q)
    z_own[...] = beside_sums(q)

    pl.semaphore_wait(barrier, len(greeted))

    first_copies = [
        copy(self_own, self_far, 21, across),
        copy(z_own, z_first.at[1, 1], 22, left_far),
        copy(z_own, z_first.at[0, 1], 23, right_far),
        copy(z_own, z_first.at[1, 0], 24, left_same),
        copy(z_own, z_first.at[0, 0], 25, right_same),
    ]
    start(first_copies)

    held_h = {1: h1, 2: h2, 3: h3}
    samples = {b: gather(own_h.at[b - 1], held_h[b], 35 + 7 * (b - 1)) for b in (1, 2, 3)}
    near, over, onward = gather(xs, xa, 0)
    for b in (1, 2, 3):
        locate(b)
        keep_sample(b)
        held_h[b][members_of(me)] = own_h[b - 1]
        samples[b][1].start()
        start(samples[b][0])

    @pl.when(jnp.logical_not(middle))
    def _():
        over.start()

    @pl.when(early_near)
    def _():
        start(near)


    xa[members_of(me)] = xs[...]

    y_of = {(0, 1): y10, (0, 2): y20, (0, 3): y30, (1, 1): y11, (1, 2): y21, (1, 3): y31, (2, 2): y22, (2, 3): y32, (3, 3): y33}
    blocks_of = {(0, 1): h1, (0, 2): h2, (0, 3): h3, (1, 2): h21, (1, 3): h31, (2, 3): h32}

    def rows_at(b, batch):
        return [y_of[b, batch][pl.ds(t, MEMBERS, stride=8), :] for t in range(OTILES)]

    def mean_rows(batch):
        return pl.ds(8 * (batch - 1), OTILES)

    def mean_row(batch, t):
        return pl.ds(8 * (batch - 1) + t, 1)

    def terms(b):
        return jnp.concatenate(
            [term(b, t, y - 0.1 * mean_h[mean_row(b, t), :]) for t, y in enumerate(rows_at(b, b))], axis=1
        )

    def evolve(b, batch):
        src, flat = blocks_of[b, batch], y_of[0, batch] if b == 0 else None
        rows, blocks = y_of[b + 1, batch], blocks_of.get((b + 1, batch))
        old = None if b == 0 else 0.11 * mean_h[mean_rows(batch), :]

        def step(m, _):
            at = pl.ds(pl.multiple_of(m * 8, 8), OTILES)
            now = src[m]
            y = 0.8 * src[anc_ref[b, 0, m]] + 0.3 * now
            y = y if old is None else y - old
            rows[at, :] = y
            if blocks is not None:
                blocks[m] = y
            if flat is not None:
                flat[at, :] = now
            return 0

        lax.fori_loop(0, MEMBERS, step, 0, unroll=8)

    def mean_at(b, batch, w_parts):
        wm = dot(w_parts, onehot[batch])
        wm = wm[:MEMBERS] + wm[MEMBERS:]
        for t, y in enumerate(rows_at(b, batch)):
            m = jnp.sum(wm[:, 128 * t : 128 * t + 128] * y, axis=0, keepdims=True)
            if b > 0:
                m = m - 0.1 * mean_h[mean_row(batch, t), :]
            mean_h[mean_row(batch, t), :] = m

    def mean_state(b, x):
        def step(i, parts):
            at = [PARTS * i + j for j in range(PARTS)]
            return tuple(part + w_all[b, pl.ds(m, 1), :] * x[m] for part, m in zip(parts, at))

        parts = lax.fori_loop(0, MEMBERS // PARTS, step, (jnp.zeros((16, CELLS), F32),) * PARTS, unroll=4)
        return (parts[0] + parts[1]) + (parts[2] + parts[3])

    def advance(b, x, y):
        mean_x[...] = 0.1 * mean_state(b, x)

        def step(m, _):
            y[m] = 0.8 * x[anc_ref[b, 0, m]] + 0.3 * x[m] - mean_x[...]
            return 0

        lax.fori_loop(0, MEMBERS, step, 0, unroll=8)

    def weigh(b, scores):
        raised = jnp.exp(scores - jnp.max(scores, axis=0, keepdims=True))
        weights = raised / jnp.sum(raised, axis=0, keepdims=True)
        w_all[b] = weights
        return jnp.concatenate(split2(weights), axis=0)

    arrive(samples[1][1:2])
    start(samples[1][2])

    arrive(first_copies)

    @pl.when(middle)
    def _():
        over.start()

    near_scores, far_scores = (
        beside_scores(0, z_first[0, i], z_first[1, i], own[...]) for i, own in enumerate((self_own, self_far))
    )
    s_out[pl.ds(0, 16), :] = near_scores
    s_out[pl.ds(OWN, OWN), :] = far_scores[:OWN]
    s_out[pl.ds(2 * OWN, 4), :] = jnp.zeros((4, CELLS), F32)
    s_copies = [copy(s_out, s_in.at[along_x], 26 + i, p) for i, p in enumerate(partners)]
    start(s_copies)
    s_in[along_x] = s_out[...]
    localize(1)
    for b in (2, 3):
        arrive(samples[b][1:2])
        start(samples[b][2])

    arrive((*samples[1][0], *samples[1][2]))
    evolve(0, 1)
    arrive(s_copies)
    @pl.when(jnp.logical_not(early_near))
    def _():
        start(near)

    for half, first in ((0, near_half), (1, 1 - near_half)):
        rows = jnp.concatenate([s_in[i, pl.ds(OWN * half, OWN), :] for i in range(ALONG_X)], axis=0)
        s_all[pl.ds(pl.multiple_of(first * (MEMBERS // 2), 8), MEMBERS // 2), :] = rows

    w_parts = weigh(0, s_all[...])
    mean_at(0, 1, w_parts)

    sent = [*first_copies, *s_copies]
    for group in samples.values():
        sent += [*group[0], group[1], *group[2]]
    for b in range(1, BATCHES):
        q = terms(b)
        z_out[b - 1] = beside_sums(q)
        halo = [
            copy(z_out.at[b - 1], z_in.at[b - 1, 1], 27 + 2 * b, left),
            copy(z_out.at[b - 1], z_in.at[b - 1, 0], 28 + 2 * b, right),
        ]
        start(halo)
        self_scores[...] = own_scores(q)

        if b == 1:
            @pl.when(early_far)
            def _():
                over.wait_recv()
                start(onward)

            arrive((*samples[2][0], *samples[2][2]))
            evolve(0, 2)
            mean_at(0, 2, w_parts)
            evolve(1, 2)
            held_w = w_parts

            @pl.when(jnp.logical_not(early_far))
            def _():
                over.wait_recv()
                start(onward)
        if b == 2:
            @pl.when(middle)
            def _():
                over.wait_recv()
                start(onward)

            arrive((*samples[3][0], *samples[3][2]))
            evolve(0, 3)
            mean_at(0, 3, held_w)
            evolve(1, 3)
            mean_at(1, 3, w_parts)
            evolve(2, 3)
        if b == 3:
            arrive((*near, *onward))
            advance(0, xa, xb)
            leave((*near, over, *onward))
            advance(1, xb, xa)
            advance(2, xa, xb)
            for i in range(OWN):
                m = me * OWN + i
                xs[i] = 0.8 * xb[anc_ref[b, 0, m]] + 0.3 * xb[m]
        if b + 1 < BATCHES:
            localize(b + 1)

        arrive(halo)
        sent += halo
        w_parts = weigh(b, beside_scores(b, z_in[b - 1, 0], z_in[b - 1, 1], self_scores[...]))
        if b + 1 < BATCHES:
            mean_at(b, b + 1, w_parts)

    mean = 0.1 * mean_state(BATCHES - 1, xb)
    for i in range(OWN):
        out_ref[i] = xs[i, pl.ds(0, VARS), :] - mean[:VARS]
    leave(sent)


def local(regions, x, observed, obs_error, obs_index, pattern, ancestors):
    whole = pl.BlockSpec(memory_space=pltpu.VMEM)
    vmem = pltpu.VMEM
    return pl.pallas_call(
        functools.partial(body, regions),
        out_shape=jax.ShapeDtypeStruct((OWN, VARS, CELLS), F32),
        in_specs=[pl.BlockSpec(memory_space=pltpu.HBM)] * 6,
        out_specs=whole,
        scratch_shapes=[
            vmem((OWN, VARS, CELLS), F32),
            vmem((BATCHES, OBS), F32),
            vmem((BATCHES, OBS), F32),
            vmem((BATCHES, OBS), jnp.int32),
            pltpu.SMEM((BATCHES, 1, 3, 2, OTILES), jnp.int32),
            pltpu.SMEM((BATCHES, 1, MEMBERS), jnp.int32),
            vmem((OWN, 16, CELLS), F32),
            vmem((2, 256, 128), F32),
            vmem((3 * 16 * VARS, CELLS), BF16),
            vmem((BATCHES, CELLS, OBS), BF16),
            vmem((BATCHES - 1, 128, 128), F32),
            vmem((BATCHES - 1, OWN, OTILES, 128), F32),
            *[vmem((8 * MEMBERS, 128), F32)] * 9,
            *[vmem((MEMBERS, OTILES, 128), F32)] * 6,
            vmem((MEMBERS, 16, CELLS), F32),
            vmem((MEMBERS, 16, CELLS), F32),
            vmem((OBS, CELLS), F32),
            vmem((OBS, 2 * CELLS), BF16),
            vmem((OBS, 2 * 128), BF16),
            vmem((2, 2 * OTILES, CELLS), F32),
            vmem((8, 128), F32),
            vmem((2, 2, 8, 128), F32),
            vmem((16, CELLS), F32),
            vmem((16, CELLS), F32),
            vmem((24, CELLS), F32),
            vmem((ALONG_X, 24, CELLS), F32),
            vmem((MEMBERS, CELLS), F32),
            vmem((BATCHES - 1, 8, 128), F32),
            vmem((BATCHES - 1, 2, 8, 128), F32),
            vmem((MEMBERS, CELLS), F32),
            vmem((BATCHES, MEMBERS, CELLS), F32),
            vmem((24, 128), F32),
            vmem((16, CELLS), F32),
            pltpu.SemaphoreType.DMA((6,)),
            pltpu.SemaphoreType.DMA((56,)),
            pltpu.SemaphoreType.DMA((56,)),
        ],
        compiler_params=pltpu.CompilerParams(
            collective_id=0, has_side_effects=True, vmem_limit_bytes=56 << 20
        ),
        name="particle_filter",
    )(x, observed, obs_error, obs_index, jnp.swapaxes(pattern, 3, 4), ancestors)


def solution(mesh):
    placed = (
        P("member", None, "region"),
        P(None, "region"),
        P(None, "region"),
        P(None, "region"),
        P(None, "region", None, None, None),
        P(None, "region", None),
    )
    return jax.shard_map(
        functools.partial(local, mesh.shape["region"]),
        mesh=mesh, in_specs=placed, out_specs=P("member", None, "region"), check_vma=False,
    )
```

```python
import functools

import jax
import jax.numpy as jnp
from jax import lax
from jax.experimental import pallas as pl
from jax.experimental.pallas import tpu as pltpu
from jax.sharding import PartitionSpec as P

MESH = pl.DeviceIdType.MESH
F32, BF16 = jnp.float32, jnp.bfloat16

BATCHES = 4
MEMBERS = 80
GROUP = 8
OWN = 10
VARS = 15
CELLS = 256
OBS = 512
OTILES = 4
ALONG_X = 4
Z_CHIPS, EARLY_FAR, EARLY_NEAR = 8, 4, 4
PARTS = 4


def split2(a):
    hi = a.astype(BF16)
    lo = (a - hi.astype(F32)).astype(BF16)
    return hi, lo


def split3(a):
    hi = a.astype(BF16)
    rest = a - hi.astype(F32)
    mid = rest.astype(BF16)
    lo = (rest - mid.astype(F32)).astype(BF16)
    return hi, mid, lo


def dot(a, b):
    return jnp.dot(a, b, preferred_element_type=F32)


def body(
    regions,
    x_hbm, obs_hbm, err_hbm, idx_hbm, pat_hbm, anc_hbm,
    out_ref,
    x_ref, obs_ref, err_ref, idx_ref, pat_ref, anc_ref,
    xs, xh, lhs, onehot, own_2d, own_h, y10, y20, y30, y11, y21, y31, y22, y32, y33,
    h1, h2, h3, h21, h31, h32, xa, xb,
    taper, loc, reach, land, z_own, z_first, self_own, self_far, s_out, s_in, s_all, z_out, z_in,
    self_scores, w_all, mean_h, mean_x,
    load_sem, send, recv,
):
    r = lax.axis_index("region")
    me = lax.axis_index("member")
    along_x = me % ALONG_X
    far = (me + ALONG_X) % GROUP
    base = me - along_x
    near_half = me // ALONG_X
    z = (r // 2) % Z_CHIPS
    early_far, last = z < EARLY_FAR, z == Z_CHIPS - 1
    middle = z < 0
    early_near = jnp.logical_and(z < EARLY_NEAR, r % (2 * Z_CHIPS) != 0)

    def beside(step):
        n = r + step
        wrapped = jnp.logical_or(n < 0, n >= regions)
        n = (n + regions) % regions
        return (n, jnp.where(wrapped, far, me)), (n, me), (n, far)

    (left, left_same, left_far), (right, right_same, right_far) = beside(-1), beside(1)
    partners = [(r, base + (along_x + d) % ALONG_X) for d in (1, 2, 3)]
    across = (r, far)

    def copy(src, dst, sem, device):
        return pltpu.make_async_remote_copy(
            src_ref=src, dst_ref=dst, send_sem=send.at[sem], recv_sem=recv.at[sem],
            device_id=device, device_id_type=MESH,
        )

    barrier = pltpu.get_barrier_semaphore()
    greeted = (across, left_same, right_same, left_far, right_far, *partners)
    for device in greeted:
        pl.semaphore_signal(barrier, inc=1, device_id=device, device_id_type=MESH)

    held = ((idx_hbm, idx_ref), (pat_hbm, pat_ref), (x_hbm, x_ref), (obs_hbm, obs_ref), (err_hbm, err_ref), (anc_hbm, anc_ref))
    loads = [pltpu.make_async_copy(src, dst, load_sem.at[i]) for i, (src, dst) in enumerate(held)]
    for c in loads:
        c.start()

    at = lax.broadcasted_iota(jnp.int32, (OBS, CELLS), 0) // 2
    column = lax.broadcasted_iota(jnp.int32, (OBS, CELLS), 1)
    taper[...] = jnp.exp(jnp.abs(at - column).astype(F32) * (-1.0 / (0.5 * CELLS)))
    at = lax.broadcasted_iota(jnp.int32, (OBS, 128), 0)
    tile = lax.broadcasted_iota(jnp.int32, (OBS, 128), 1) % (2 * OTILES)
    away = jnp.where(tile < OTILES, at // 2, CELLS - at // 2).astype(F32)
    held_by = tile % OTILES == at // 128
    reach[:, :128], reach[:, 128:] = split2(jnp.where(held_by, jnp.exp(away * (-1.0 / (0.5 * CELLS))), 0.0))
    for zeroed in (xs, xh):
        zeroed[...] = jnp.zeros_like(zeroed)

    def locate(b):
        where = idx_ref[pl.ds(b, 1), :]
        rows = lax.broadcasted_iota(jnp.int32, (CELLS, OBS), 0)
        hot = jnp.where(rows == where % CELLS, 1.0, 0.0).astype(BF16)
        onehot[b, :CELLS], onehot[b, CELLS:] = hot, hot

    lane = lax.broadcasted_iota(jnp.int32, (1, CELLS), 1)

    def blocks(b, k, t):
        low, high = (pat_ref[b, 0, k, c, t].astype(F32) for c in (0, 1))
        return jnp.where(lane < 128, low, high)

    def localize(b):
        for t in range(OTILES):
            rows = pl.ds(128 * t, 128)
            loc[rows, :CELLS], loc[rows, CELLS:] = split2(taper[rows, :] * blocks(b, 1, t))
        lands = []
        for k, gap in ((2, CELLS - lane), (0, lane)):
            factor = jnp.exp(gap.astype(F32) * (-1.0 / (0.5 * CELLS)))
            lands += [factor * blocks(b, k, t) for t in range(OTILES)]
        land[b % 2] = jnp.concatenate(lands, axis=0)

    def product(a, b):
        n, k = a.shape[0], b.shape[1] // 2
        all_four = dot(jnp.concatenate(split2(a), axis=0), b)
        return all_four[:n, :k] + (all_four[n:, :k] + all_four[:n, k:]) + all_four[n:, k:]

    def own_scores(q):
        return product(q, loc[...])

    def beside_sums(q):
        sums = product(q, reach[...])
        held = lax.broadcasted_iota(jnp.int32, (8, 128), 1) // 8
        packed = jnp.zeros((8, 128), F32)
        for g in range(q.shape[0] // 8):
            packed = jnp.where(held == g, sums[8 * g : 8 * g + 8], packed)
        return packed

    def beside_scores(b, from_left, from_right, start):
        found = []
        for g in range(start.shape[0] // 8):
            total = start[8 * g : 8 * g + 8]
            for i in range(2 * OTILES):
                sums = (from_right if i < OTILES else from_left)[:, 8 * g + i : 8 * g + i + 1]
                total = total + sums * land[b % 2, pl.ds(i, 1), :]
            found.append(total)
        return jnp.concatenate(found, axis=0)

    loads[0].wait()
    locate(0)
    loads[1].wait()
    localize(0)
    loads[2].wait()
    for m in range(OWN):
        x = x_ref[m]
        xs[m, pl.ds(0, VARS), :] = x
        for half in (0, 1):
            xh[half, pl.ds(16 * m, VARS), :] = x[:, 128 * half : 128 * half + 128]
    for v in range(VARS):
        x = jnp.concatenate([xh[half, pl.ds(v, 16, stride=16), :] for half in (0, 1)], axis=1)
        for part, piece in enumerate(split3(x)):
            lhs[pl.ds(part * 16 * VARS + 16 * v, 16), :] = piece

    def sample(b):
        var = idx_ref[pl.ds(b, 1), :] // CELLS
        got = dot(lhs[...], onehot[b, :CELLS])
        n = 16 * VARS
        got = got[:n] + got[n : 2 * n] + got[2 * n :]
        total = jnp.zeros((16, OBS), F32)
        for v in range(VARS):
            total = total + jnp.where(var == v, got[16 * v : 16 * v + 16], 0.0)
        return total

    def keep_sample(b):
        total = sample(b)
        for t in range(OTILES):
            own_2d[b - 1, pl.ds(t, 16, stride=8), :] = total[:, 128 * t : 128 * t + 128]
        for m in range(OWN):
            own_h[b - 1, m] = own_2d[b - 1, pl.ds(8 * m, OTILES), :]

    def term(b, t, y):
        lanes = pl.ds(128 * t, 128)
        miss = obs_ref[pl.ds(b, 1), lanes] - y
        err = err_ref[pl.ds(b, 1), lanes]
        return -(miss * miss) * (0.5 / (err * err))

    def members_of(member):
        return pl.ds(member * OWN, OWN)

    def gather(src, dst, sem):
        mine, theirs = dst.at[members_of(me)], dst.at[members_of(far)]
        near = [copy(src, mine, sem + i, p) for i, p in enumerate(partners)]
        over = copy(src, mine, sem + 3, across)
        onward = [copy(theirs, theirs, sem + 4 + i, p) for i, p in enumerate(partners)]
        return near, over, onward

    def start(copies):
        for c in copies:
            c.start()

    def arrive(copies):
        for c in copies:
            c.wait_recv()

    def leave(copies):
        for c in copies:
            c.wait_send()

    for c in loads[3:]:
        c.wait()
    first = sample(0)
    q = jnp.concatenate([term(0, t, first[:, 128 * t : 128 * t + 128]) for t in range(OTILES)], axis=1)
    self_own[...] = own_scores(q)
    z_own[...] = beside_sums(q)

    pl.semaphore_wait(barrier, len(greeted))

    first_copies = [
        copy(self_own, self_far, 21, across),
        copy(z_own, z_first.at[1, 1], 22, left_far),
        copy(z_own, z_first.at[0, 1], 23, right_far),
        copy(z_own, z_first.at[1, 0], 24, left_same),
        copy(z_own, z_first.at[0, 0], 25, right_same),
    ]
    start(first_copies)

    held_h = {1: h1, 2: h2, 3: h3}
    samples = {b: gather(own_h.at[b - 1], held_h[b], 35 + 7 * (b - 1)) for b in (1, 2, 3)}
    near, over, onward = gather(xs, xa, 0)
    for b in (1, 2, 3):
        locate(b)
        keep_sample(b)
        held_h[b][members_of(me)] = own_h[b - 1]
        samples[b][1].start()
        start(samples[b][0])

    @pl.when(jnp.logical_not(middle))
    def _():
        over.start()

    @pl.when(early_near)
    def _():
        start(near)


    xa[members_of(me)] = xs[...]

    y_of = {(0, 1): y10, (0, 2): y20, (0, 3): y30, (1, 1): y11, (1, 2): y21, (1, 3): y31, (2, 2): y22, (2, 3): y32, (3, 3): y33}
    blocks_of = {(0, 1): h1, (0, 2): h2, (0, 3): h3, (1, 2): h21, (1, 3): h31, (2, 3): h32}

    def rows_at(b, batch):
        return [y_of[b, batch][pl.ds(t, MEMBERS, stride=8), :] for t in range(OTILES)]

    def mean_rows(batch):
        return pl.ds(8 * (batch - 1), OTILES)

    def mean_row(batch, t):
        return pl.ds(8 * (batch - 1) + t, 1)

    def terms(b):
        return jnp.concatenate(
            [term(b, t, y - 0.1 * mean_h[mean_row(b, t), :]) for t, y in enumerate(rows_at(b, b))], axis=1
        )

    def evolve(b, batch):
        src, flat = blocks_of[b, batch], y_of[0, batch] if b == 0 else None
        rows, blocks = y_of[b + 1, batch], blocks_of.get((b + 1, batch))
        old = None if b == 0 else 0.11 * mean_h[mean_rows(batch), :]

        def step(m, _):
            at = pl.ds(pl.multiple_of(m * 8, 8), OTILES)
            now = src[m]
            y = 0.8 * src[anc_ref[b, 0, m]] + 0.3 * now
            y = y if old is None else y - old
            rows[at, :] = y
            if blocks is not None:
                blocks[m] = y
            if flat is not None:
                flat[at, :] = now
            return 0

        lax.fori_loop(0, MEMBERS, step, 0, unroll=8)

    def mean_at(b, batch, w_parts):
        wm = dot(w_parts, onehot[batch])
        for t, y in enumerate(rows_at(b, batch)):
            m = jnp.sum(wm[:, 128 * t : 128 * t + 128] * y, axis=0, keepdims=True)
            if b > 0:
                m = m - 0.1 * mean_h[mean_row(batch, t), :]
            mean_h[mean_row(batch, t), :] = m

    def mean_state(b, x):
        def step(i, parts):
            at = [PARTS * i + j for j in range(PARTS)]
            return tuple(part + w_all[b, pl.ds(m, 1), :] * x[m] for part, m in zip(parts, at))

        parts = lax.fori_loop(0, MEMBERS // PARTS, step, (jnp.zeros((16, CELLS), F32),) * PARTS, unroll=4)
        return (parts[0] + parts[1]) + (parts[2] + parts[3])

    def advance(b, x, y):
        mean_x[...] = 0.1 * mean_state(b, x)

        def step(m, _):
            y[m] = 0.8 * x[anc_ref[b, 0, m]] + 0.3 * x[m] - mean_x[...]
            return 0

        lax.fori_loop(0, MEMBERS, step, 0, unroll=8)

    def weigh(b, scores):
        raised = jnp.exp(scores - jnp.max(scores, axis=0, keepdims=True))
        weights = raised / jnp.sum(raised, axis=0, keepdims=True)
        w_all[b] = weights
        return jnp.concatenate(split2(weights), axis=1)

    arrive(samples[1][1:2])
    start(samples[1][2])

    arrive(first_copies)

    @pl.when(middle)
    def _():
        over.start()

    near_scores, far_scores = (
        beside_scores(0, z_first[0, i], z_first[1, i], own[...]) for i, own in enumerate((self_own, self_far))
    )
    s_out[pl.ds(0, 16), :] = near_scores
    s_out[pl.ds(OWN, OWN), :] = far_scores[:OWN]
    s_out[pl.ds(2 * OWN, 4), :] = jnp.zeros((4, CELLS), F32)
    s_copies = [copy(s_out, s_in.at[along_x], 26 + i, p) for i, p in enumerate(partners)]
    start(s_copies)
    s_in[along_x] = s_out[...]
    localize(1)
    for b in (2, 3):
        arrive(samples[b][1:2])
        start(samples[b][2])

    arrive((*samples[1][0], *samples[1][2]))
    evolve(0, 1)
    arrive(s_copies)
    @pl.when(jnp.logical_not(early_near))
    def _():
        start(near)

    for half, first in ((0, near_half), (1, 1 - near_half)):
        rows = jnp.concatenate([s_in[i, pl.ds(OWN * half, OWN), :] for i in range(ALONG_X)], axis=0)
        s_all[pl.ds(pl.multiple_of(first * (MEMBERS // 2), 8), MEMBERS // 2), :] = rows

    w_parts = weigh(0, s_all[...])
    mean_at(0, 1, w_parts)

    sent = [*first_copies, *s_copies]
    for group in samples.values():
        sent += [*group[0], group[1], *group[2]]
    for b in range(1, BATCHES):
        q = terms(b)
        z_out[b - 1] = beside_sums(q)
        halo = [
            copy(z_out.at[b - 1], z_in.at[b - 1, 1], 27 + 2 * b, left),
            copy(z_out.at[b - 1], z_in.at[b - 1, 0], 28 + 2 * b, right),
        ]
        start(halo)
        self_scores[...] = own_scores(q)

        if b == 1:
            @pl.when(early_far)
            def _():
                over.wait_recv()
                start(onward)

            arrive((*samples[2][0], *samples[2][2]))
            evolve(0, 2)
            mean_at(0, 2, w_parts)
            evolve(1, 2)
            held_w = w_parts

            @pl.when(jnp.logical_not(early_far))
            def _():
                over.wait_recv()
                start(onward)
        if b == 2:
            @pl.when(middle)
            def _():
                over.wait_recv()
                start(onward)

            arrive((*samples[3][0], *samples[3][2]))
            evolve(0, 3)
            mean_at(0, 3, held_w)
            evolve(1, 3)
            mean_at(1, 3, w_parts)
            evolve(2, 3)
        if b == 3:
            arrive((*near, *onward))
            advance(0, xa, xb)
            leave((*near, over, *onward))
            advance(1, xb, xa)
            advance(2, xa, xb)
            for i in range(OWN):
                m = me * OWN + i
                xs[i] = 0.8 * xb[anc_ref[b, 0, m]] + 0.3 * xb[m]
        if b + 1 < BATCHES:
            localize(b + 1)

        arrive(halo)
        sent += halo
        w_parts = weigh(b, beside_scores(b, z_in[b - 1, 0], z_in[b - 1, 1], self_scores[...]))
        if b + 1 < BATCHES:
            mean_at(b, b + 1, w_parts)

    mean = 0.1 * mean_state(BATCHES - 1, xb)
    for i in range(OWN):
        out_ref[i] = xs[i, pl.ds(0, VARS), :] - mean[:VARS]
    leave(sent)


def local(regions, x, observed, obs_error, obs_index, pattern, ancestors):
    whole = pl.BlockSpec(memory_space=pltpu.VMEM)
    vmem = pltpu.VMEM
    return pl.pallas_call(
        functools.partial(body, regions),
        out_shape=jax.ShapeDtypeStruct((OWN, VARS, CELLS), F32),
        in_specs=[pl.BlockSpec(memory_space=pltpu.HBM)] * 6,
        out_specs=whole,
        scratch_shapes=[
            vmem((OWN, VARS, CELLS), F32),
            vmem((BATCHES, OBS), F32),
            vmem((BATCHES, OBS), F32),
            vmem((BATCHES, OBS), jnp.int32),
            pltpu.SMEM((BATCHES, 1, 3, 2, OTILES), jnp.int32),
            pltpu.SMEM((BATCHES, 1, MEMBERS), jnp.int32),
            vmem((OWN, 16, CELLS), F32),
            vmem((2, 256, 128), F32),
            vmem((3 * 16 * VARS, CELLS), BF16),
            vmem((BATCHES, 2 * CELLS, OBS), BF16),
            vmem((BATCHES - 1, 128, 128), F32),
            vmem((BATCHES - 1, OWN, OTILES, 128), F32),
            *[vmem((8 * MEMBERS, 128), F32)] * 9,
            *[vmem((MEMBERS, OTILES, 128), F32)] * 6,
            vmem((MEMBERS, 16, CELLS), F32),
            vmem((MEMBERS, 16, CELLS), F32),
            vmem((OBS, CELLS), F32),
            vmem((OBS, 2 * CELLS), BF16),
            vmem((OBS, 2 * 128), BF16),
            vmem((2, 2 * OTILES, CELLS), F32),
            vmem((8, 128), F32),
            vmem((2, 2, 8, 128), F32),
            vmem((16, CELLS), F32),
            vmem((16, CELLS), F32),
            vmem((24, CELLS), F32),
            vmem((ALONG_X, 24, CELLS), F32),
            vmem((MEMBERS, CELLS), F32),
            vmem((BATCHES - 1, 8, 128), F32),
            vmem((BATCHES - 1, 2, 8, 128), F32),
            vmem((MEMBERS, CELLS), F32),
            vmem((BATCHES, MEMBERS, CELLS), F32),
            vmem((24, 128), F32),
            vmem((16, CELLS), F32),
            pltpu.SemaphoreType.DMA((6,)),
            pltpu.SemaphoreType.DMA((56,)),
            pltpu.SemaphoreType.DMA((56,)),
        ],
        compiler_params=pltpu.CompilerParams(
            collective_id=0, has_side_effects=True, vmem_limit_bytes=56 << 20
        ),
        name="particle_filter",
    )(x, observed, obs_error, obs_index, jnp.swapaxes(pattern, 3, 4), ancestors)


def solution(mesh):
    placed = (
        P("member", None, "region"),
        P(None, "region"),
        P(None, "region"),
        P(None, "region"),
        P(None, "region", None, None, None),
        P(None, "region", None),
    )
    return jax.shard_map(
        functools.partial(local, mesh.shape["region"]),
        mesh=mesh, in_specs=placed, out_specs=P("member", None, "region"), check_vma=False,
    )
```
